256 devices in a mesh: scan: 32 (over z_hi, x, core), band: 8 (over z_lo, y).
Axes of the slice: x: 4, y: 4, z: 8 (z_hi: 4, z_lo: 2; z = z_hi * 2 + z_lo), core: 2. Of those that a mesh axis runs over, the one named last changes fastest.
Arguments:
- frame_codes: bfloat16 [2048, 576, 576], P('scan', 'band'), may hold values from 0.049804688 to 1
- row_scales: float32 [2048, 576], P('scan', 'band'), may hold values from 0.3 to 9
- row_shift: int32 [2048], P('scan'), may hold values from -9 to 9
- col_shift: int32 [2048], P('scan'), may hold values from -72 to 72
- segment_labels: int32 [576, 576], P('band'), may hold values from 0 to 127, as said below
- mask_coeffs: float32 [3, 128, 512], replicated, may hold values from -72 to 72
Outputs:
- virtual: float32 [2048, 512], P('scan', 'band')
The draws below stay inside these ranges and needn't reach their ends.
Inputs may be any that keep to these rules, and one draw needn't show every extreme that they name: `segment_labels`: every segment number occurs.
All inputs are finite; a program needn't handle non-finite values.
Results may differ from the reference program's by a relative error of at most 0.0003.
Values may be sent and summed in bfloat16 or wider, within the bound.
No kernel may reach another device: no remote copies, remote signals or barrier semaphores. Data moves between devices by JAX's collectives and lax.ppermute only.
A program may use at most 192 MiB of HBM per device.

```python
import jax
import jax.numpy as jnp
from jax import lax

DET = 576
MASKS = 512
SEGS = 128
FR_DEV = 64
FRAMES = 2048
SHIFT = 9
CSHIFT = 72
N_SCAN = 32


def bounded_shifts(key, total, limit):
    values = jax.random.randint(key, (total,), -limit, limit + 1)
    spots = jax.random.permutation(jax.random.fold_in(key, 7), total)
    values = values.at[spots[0]].set(limit)
    values = values.at[spots[1]].set(-limit)
    return values.astype(jnp.int32)


def draw_row_shift(key, part):
    key = jax.random.fold_in(key, 11)
    return bounded_shifts(key, FRAMES, SHIFT)


def draw_col_shift(key, part):
    key = jax.random.fold_in(key, 12)
    return bounded_shifts(key, FRAMES, CSHIFT)


def draw_segment_labels(key, part):
    key = jax.random.fold_in(key, 13)
    centre = jax.random.randint(key, (2,), DET // 2 - DET // 16, DET // 2 + DET // 16 + 1)
    offset_y = jnp.arange(DET, dtype=jnp.int32)[:, None] - centre[0]
    offset_x = jnp.arange(DET, dtype=jnp.int32)[None, :] - centre[1]
    radius_sq = offset_y * offset_y + offset_x * offset_x
    cycle = jnp.minimum(15, radius_sq * 16 // (DET * DET // 4))
    octant = (offset_x >= 0).astype(jnp.int32) * 4 + (offset_y >= 0).astype(jnp.int32) * 2 + (jnp.abs(offset_x) >= jnp.abs(offset_y)).astype(jnp.int32)
    order = jax.random.permutation(jax.random.fold_in(key, 5), SEGS).astype(jnp.int32)
    return order[cycle * 8 + octant].astype(jnp.int32)


def draw_row_scales(key, part):
    key = jax.random.fold_in(key, 14)
    ramp = 1.0 + 2.0 * jnp.arange(FRAMES, dtype=jnp.float32) / (FRAMES - 1)
    base = jax.random.uniform(key, (FRAMES, DET), jnp.float32, 0.5, 1.5)
    return (base * ramp[:, None]).astype(jnp.float32)


def shard_levels(key, shape, pieces, smallest, largest):
    loudness, own = 1.0, jax.random.fold_in(key, 6)
    for axis_at, blocks in pieces:
        draws = jnp.exp(jax.random.uniform(jax.random.fold_in(own, axis_at), (blocks,), jnp.float32, smallest / len(pieces), largest / len(pieces)))
        loudness = loudness * jnp.repeat(draws, shape[axis_at] // blocks).reshape([-1 if axis == axis_at else 1 for axis in range(len(shape))])
    return loudness


def scatter_about(own_key, dims, spread, bound, held_as=jnp.bfloat16):
    return jnp.clip(spread * jax.random.normal(own_key, dims, jnp.float32), -bound, bound).astype(held_as)


def setup_inputs(seed: int = 0) -> dict:
    arg_keys = jax.random.split(jax.random.key(seed), 7)
    return {
        "frame_codes": jnp.clip(0.049804688 + 0.9501953 * jax.random.uniform(arg_keys[0], (FRAMES, DET, DET), jnp.float32) ** shard_levels(arg_keys[0], (FRAMES, DET, DET), ((0, 32), (1, 8)), -0.2, 0.2), 0.049804688, 1.0).astype(jnp.bfloat16),
        "row_scales": draw_row_scales(jax.random.fold_in(arg_keys[6], 71), 0),
        "row_shift": draw_row_shift(jax.random.fold_in(arg_keys[6], 71), 0),
        "col_shift": draw_col_shift(jax.random.fold_in(arg_keys[6], 71), 0),
        "segment_labels": draw_segment_labels(jax.random.fold_in(arg_keys[6], 71), 0),
        "mask_coeffs": scatter_about(arg_keys[5], (3, SEGS, MASKS), 12.0, 72.0, jnp.float32),
    }


def basis_table(labels, first_row):
    row_total, col_total = labels.shape
    global_rows = first_row + jnp.arange(row_total, dtype=jnp.int32)
    inside = ((global_rows >= 0) & (global_rows < DET)).astype(jnp.float32)
    ycoord = (global_rows.astype(jnp.float32) + 0.5) / DET - 0.5
    xcoord = (jnp.arange(col_total, dtype=jnp.int32).astype(jnp.float32) + 0.5) / DET - 0.5
    plane = jnp.ones((row_total, col_total), jnp.float32) * inside[:, None]
    basis = jnp.stack([plane, plane * ycoord[:, None], plane * xcoord[None, :]], axis=-1).astype(jnp.bfloat16)
    onehot = (labels[:, :, None] == jnp.arange(SEGS, dtype=jnp.int32)).astype(jnp.bfloat16)
    table = basis[:, :, :, None] * onehot[:, :, None, :]
    return table.reshape(row_total * col_total, 3 * SEGS)


def select_window(single, row_step, col_step):
    starts = (SHIFT - row_step).astype(jnp.int32), (CSHIFT - col_step).astype(jnp.int32)
    return lax.dynamic_slice(single, starts, (DET, DET))


def reference(frame_codes, row_scales, row_shift, col_shift, segment_labels, mask_coeffs):
    dequant = (frame_codes.astype(jnp.float32) * row_scales[:, :, None]).astype(jnp.bfloat16)
    table = basis_table(segment_labels, 0)

    def block_sums(items):
        frames, row_steps, col_steps = items
        padded = jnp.pad(frames, ((0, 0), (SHIFT, SHIFT), (CSHIFT, CSHIFT)))
        moved = jax.vmap(select_window)(padded, row_steps, col_steps)
        return jnp.dot(moved.reshape(FR_DEV, DET * DET), table, preferred_element_type=jnp.float32)

    moments = lax.map(block_sums, (dequant.reshape(N_SCAN, FR_DEV, DET, DET), row_shift.reshape(N_SCAN, FR_DEV), col_shift.reshape(N_SCAN, FR_DEV)))
    moments = moments.reshape(FRAMES, 3 * SEGS)
    mean_total = jnp.sum(moments[:, :SEGS]) / FRAMES
    weights = mask_coeffs.reshape(3 * SEGS, MASKS)
    return jnp.dot(moments, weights, precision=lax.Precision.HIGHEST, preferred_element_type=jnp.float32) / mean_total
```

```python
import functools

import jax
import jax.numpy as jnp
from jax import lax
from jax.experimental import pallas as pl
from jax.experimental.pallas import tpu as pltpu
from jax.sharding import PartitionSpec as P

MASKS = 512
SEGS = 128
LANES = 128
MIB = 2**20
VMEM = pl.BlockSpec(memory_space=pltpu.VMEM)
SMEM = pl.BlockSpec(memory_space=pltpu.SMEM)


class Sizes:
    def __init__(self, frame_count, band_height, det_cols):
        self.frames = frame_count
        self.rows = band_height
        self.cols = det_cols
        self.reach = band_height // 8
        self.ext = band_height + 2 * self.reach
        self.tiles = -(-det_cols // LANES)
        self.width = self.tiles * LANES
        self.pitch = frame_count + 8


def shift_kernel(size, row_shift, col_shift, scales, codes, moved, total, split, spread, acc):
    frames, rows, cols, tiles = size.frames, size.rows, size.cols, size.tiles
    empty = jnp.zeros((frames, LANES), jnp.float32)

    def clear(e, carry):
        for t in range(tiles):
            moved[t, pl.ds(pl.multiple_of(e * size.pitch, 8), frames), :] = empty
            moved[t, pl.ds(pl.multiple_of((e + rows) * size.pitch, 8), frames), :] = empty
        return carry

    lax.fori_loop(0, 2 * size.reach, clear, 0, unroll=3)

    scale = jnp.concatenate(
        [scales[...], jnp.zeros((frames, LANES - rows), jnp.float32)], axis=1
    )
    high = scale.astype(jnp.bfloat16).astype(jnp.float32)
    middle = (scale - high).astype(jnp.bfloat16).astype(jnp.float32)
    split[0:frames, :] = high
    split[frames : 2 * frames, :] = middle
    split[2 * frames : 3 * frames, :] = scale - high - middle
    acc[...] = jnp.zeros((rows, LANES), jnp.float32)

    lane = lax.broadcasted_iota(jnp.int32, (rows, LANES), 1)
    row = lax.broadcasted_iota(jnp.int32, (rows, LANES), 0)
    diagonal = lane == row
    ones = jnp.ones((3 * LANES, LANES), jnp.bfloat16)
    zero = jnp.zeros((rows, LANES), jnp.float32)
    first_row = lax.axis_index("band") * rows

    def spread_frame(f, carry):
        parts = [
            jnp.where(
                diagonal,
                jnp.broadcast_to(split[pl.ds(f + k * frames, 1), :], (rows, LANES)),
                0.0,
            ).astype(jnp.bfloat16)
            for k in range(3)
        ]
        spread[pl.ds(pl.multiple_of(f * rows, 8), rows), :] = jnp.dot(
            jnp.concatenate(parts, axis=1), ones, preferred_element_type=jnp.float32
        )
        return carry

    lax.fori_loop(0, frames, spread_frame, 0, unroll=16)

    def shift_frame(f, carry):
        down, right = row_shift[f], col_shift[f]
        turn = jnp.where(right < 0, right + LANES, right)
        positive = right >= 0
        below = lane < turn
        from_left = below & positive
        from_right = jnp.logical_not(below | positive)
        scale_f = spread[pl.ds(pl.multiple_of(f * rows, 8), rows), :]
        turned = [zero]
        for t in range(tiles):
            upper = min(cols, (t + 1) * LANES)
            value = codes[f, :, t * LANES : upper].astype(jnp.float32)
            if upper < (t + 1) * LANES:
                fill = jnp.zeros((rows, (t + 1) * LANES - upper), jnp.float32)
                value = jnp.concatenate([value, fill], axis=1)
            dequant = (value * scale_f).astype(jnp.bfloat16).astype(jnp.float32)
            turned.append(pltpu.roll(dequant, turn, 1))
        turned.append(zero)
        start = (size.reach + down) * size.pitch + f
        row_sum = zero
        for t in range(tiles):
            out = jnp.where(
                from_left, turned[t], jnp.where(from_right, turned[t + 2], turned[t + 1])
            )
            if (t + 1) * LANES > cols:
                out = jnp.where(lane < cols - t * LANES, out, 0.0)
            moved[t, pl.ds(start, rows, stride=size.pitch), :] = out
            row_sum = row_sum + out
        target = row + (first_row + down)
        acc[...] += jnp.where((target >= 0) & (target < cols), row_sum, 0.0)
        return carry

    lax.fori_loop(0, frames, shift_frame, 0, unroll=4)
    total[...] = jnp.sum(acc[...].reshape(rows // 8, 8, LANES), axis=0)


def shift_frames(size, row_shift, col_shift, scales, codes):
    return pl.pallas_call(
        functools.partial(shift_kernel, size),
        out_shape=[
            jax.ShapeDtypeStruct((size.tiles, size.ext * size.pitch, LANES), jnp.float32),
            jax.ShapeDtypeStruct((8, LANES), jnp.float32),
        ],
        in_specs=[SMEM, SMEM, VMEM, VMEM],
        out_specs=[VMEM, VMEM],
        scratch_shapes=[
            pltpu.VMEM((3 * size.frames, LANES), jnp.float32),
            pltpu.VMEM((size.frames * size.rows, LANES), jnp.float32),
            pltpu.VMEM((size.rows, LANES), jnp.float32),
        ],
        compiler_params=pltpu.CompilerParams(vmem_limit_bytes=16 * MIB),
        cost_estimate=pl.CostEstimate(flops=4 * 10**9, bytes_accessed=10**6, transcendentals=0),
        name="shift",
    )(row_shift, col_shift, scales, codes)


def table_consts(size):
    segment = lax.broadcasted_iota(jnp.int32, (16, size.width), 0)
    column = lax.broadcasted_iota(jnp.int32, (16, size.width), 1).astype(jnp.float32)
    xcoord = ((column + 0.5) / size.cols - 0.5).astype(jnp.bfloat16)
    ids = [
        (segment + 16 * k).astype(jnp.float32).astype(jnp.bfloat16) for k in range(SEGS // 16)
    ]
    return ids, xcoord


def add_row(size, consts, label_row, moved, moments, e):
    ids, xcoord = consts
    frames = size.frames
    zero = jnp.zeros((16, size.width), jnp.bfloat16)
    one = jnp.ones((16, size.width), jnp.bfloat16)
    label = jnp.broadcast_to(label_row, (16, size.width)).astype(jnp.bfloat16)
    plain, by_x = [], []
    for k in range(SEGS // 16):
        same = label == ids[k]
        plain.append(jnp.where(same, one, zero))
        by_x.append(jnp.where(same, xcoord, zero))
    table = jnp.concatenate(plain + by_x, axis=0)
    base = pl.multiple_of(e * size.pitch, 8)
    values = jnp.concatenate(
        [moved[t, pl.ds(base, frames), :].astype(jnp.bfloat16) for t in range(size.tiles)], axis=1
    )
    sums = lax.dot_general(
        table, values, (((1,), (1,)), ((), ())), preferred_element_type=jnp.float32
    )
    first_row = lax.axis_index("band") * size.rows
    offset = (first_row + e - size.reach).astype(jnp.float32)
    ycoord = ((offset + 0.5) / size.cols - 0.5).astype(jnp.bfloat16).astype(jnp.float32)
    moments[0:SEGS, :] += sums[0:SEGS]
    moments[SEGS : 2 * SEGS, :] += sums[0:SEGS] * ycoord
    moments[2 * SEGS : 3 * SEGS, :] += sums[SEGS : 2 * SEGS]


def widen(size, labels, out, at, count, start):
    rows = labels[pl.ds(start, count), :].astype(jnp.float32)
    fill = jnp.full((count, size.width - size.cols), -1.0, jnp.float32)
    out[pl.ds(at, count), :] = jnp.concatenate([rows, fill], axis=1)


def core_kernel(size, first, last, started, *refs):
    if started:
        labels, moved, before, moments, wide = refs
        moments[...] = before[...]
    else:
        labels, moved, moments, wide = refs
        moments[...] = jnp.zeros(moments.shape, jnp.float32)
    widen(size, labels, wide, 0, size.rows, 0)
    consts = table_consts(size)

    def step(r, carry):
        add_row(size, consts, wide[pl.ds(r, 1), :], moved, moments, r + size.reach)
        return carry

    lax.fori_loop(first, last, step, 0, unroll=12)


def core_rows(size, labels, moved, before, first, last):
    args = [labels, moved] + ([] if before is None else [before])
    return pl.pallas_call(
        functools.partial(core_kernel, size, first, last, before is not None),
        out_shape=jax.ShapeDtypeStruct((3 * SEGS, size.frames), jnp.float32),
        in_specs=[VMEM] * len(args),
        out_specs=VMEM,
        scratch_shapes=[pltpu.VMEM((size.rows, size.width), jnp.float32)],
        compiler_params=pltpu.CompilerParams(vmem_limit_bytes=8 * MIB),
        cost_estimate=pl.CostEstimate(flops=3 * 10**9, bytes_accessed=10**6, transcendentals=0),
        name="core",
    )(*args)


def edge_kernel(size, above, under, moved, before, coeffs, intensity, out, wide, moments):
    reach, frames = size.reach, size.frames
    moments[...] = before[...]
    widen(size, above, wide, 0, reach, size.rows - reach)
    widen(size, under, wide, reach, reach, 0)
    band, bands = lax.axis_index("band"), lax.axis_size("band")

    @pl.when(band == 0)
    def _():
        wide[0:reach, :] = jnp.full((reach, size.width), -1.0, jnp.float32)

    @pl.when(band == bands - 1)
    def _():
        wide[reach : 2 * reach, :] = jnp.full((reach, size.width), -1.0, jnp.float32)

    consts = table_consts(size)

    def step(r, carry):
        e = jnp.where(r < reach, r, r + size.rows)
        add_row(size, consts, wide[pl.ds(r, 1), :], moved, moments, e)
        return carry

    lax.fori_loop(0, 2 * reach, step, 0, unroll=9)
    partial = jnp.dot(
        moments[...].T,
        coeffs[...],
        precision=lax.Precision.HIGHEST,
        preferred_element_type=jnp.float32,
    )
    half = frames // 2
    width = MASKS // bands
    per = LANES // width
    lane = lax.broadcasted_iota(jnp.int32, (half, LANES), 1)
    for b in range(bands):
        at = (b // per) * LANES
        low = partial[:half, at : at + LANES]
        high = partial[half:, at : at + LANES]
        if b % per == 0:
            high = pltpu.roll(high, width, 1)
        else:
            low = pltpu.roll(low, width, 1)
        out[b, 0:half, :] = jnp.where(lane < width, low, high)
        out[b, half : half + 8, :] = intensity[...]


def edge_rows(size, above, under, moved, before, coeffs, intensity):
    bands = lax.axis_size("band")
    return pl.pallas_call(
        functools.partial(edge_kernel, size),
        out_shape=jax.ShapeDtypeStruct((bands, size.frames // 2 + 8, LANES), jnp.float32),
        in_specs=[VMEM] * 6,
        out_specs=VMEM,
        scratch_shapes=[
            pltpu.VMEM((2 * size.reach, size.width), jnp.float32),
            pltpu.VMEM((3 * SEGS, size.frames), jnp.float32),
        ],
        compiler_params=pltpu.CompilerParams(vmem_limit_bytes=12 * MIB),
        cost_estimate=pl.CostEstimate(flops=3 * 10**9, bytes_accessed=10**6, transcendentals=0),
        name="edge",
    )(above, under, moved, before, coeffs, intensity)


def finish_kernel(frame_total, blocks, out):
    bands, height, _ = blocks.shape
    half = height - 8
    summed = blocks[0]
    for b in range(1, bands):
        summed = summed + blocks[b]
    mean_total = jnp.sum(summed[half:, :]) / frame_total
    scaled = summed[:half] / mean_total
    width = out.shape[1]
    out[0:half, :] = scaled[:, :width]
    out[half:, :] = scaled[:, width:]


def finish(blocks, frame_count):
    half = frame_count // 2
    return pl.pallas_call(
        functools.partial(finish_kernel, float(frame_count * lax.axis_size("scan"))),
        out_shape=jax.ShapeDtypeStruct((2 * half, LANES // 2), jnp.float32),
        in_specs=[VMEM],
        out_specs=VMEM,
        compiler_params=pltpu.CompilerParams(vmem_limit_bytes=8 * MIB),
        name="finish",
    )(blocks)


def scan_pairs():
    count = lax.axis_size("scan")
    around = {0: 3, 1: 2, 2: 1, 3: 0}

    def z_around(i):
        return around[i // 8] * 8 + i % 8

    def x_around(i):
        return (i // 8) * 8 + around[i // 2 % 4] * 2 + i % 2

    moves = [lambda i: i ^ 8, z_around, lambda i: i ^ 2, x_around, lambda i: i ^ 1]
    return [[(i, move(i)) for i in range(count)] for move in moves]


def body(frame_codes, row_scales, row_shift, col_shift, segment_labels, mask_coeffs):
    frame_count, band_height, det_cols = frame_codes.shape
    size = Sizes(frame_count, band_height, det_cols)
    bands = lax.axis_size("band")
    down = [(i, i + 1) for i in range(bands - 1)]
    up = [(i + 1, i) for i in range(bands - 1)]
    above = lax.ppermute(segment_labels, "band", down)
    under = lax.ppermute(segment_labels, "band", up)
    moved, intensity = shift_frames(size, row_shift, col_shift, row_scales, frame_codes)
    moments = None
    third = band_height // 3
    pieces = [(0, third), (third, 2 * third), (2 * third, band_height)]
    for pairs in scan_pairs():
        intensity = intensity + lax.ppermute(intensity, "scan", pairs)
    for first, last in pieces:
        moments = core_rows(size, segment_labels, moved, moments, first, last)
    coeffs = mask_coeffs.reshape(3 * SEGS, MASKS)
    send = edge_rows(size, above, under, moved, moments, coeffs, intensity)
    blocks = lax.all_to_all(send, "band", 0, 0)
    return finish(blocks, frame_count)


def solution(mesh):
    return jax.shard_map(
        body,
        mesh=mesh,
        in_specs=(
            P("scan", "band", None),
            P("scan", "band"),
            P("scan"),
            P("scan"),
            P("band", None),
            P(),
        ),
        out_specs=P("scan", "band"),
        check_vma=False,
    )
```

```python
import functools

import jax
import jax.numpy as jnp
from jax import lax
from jax.experimental import pallas as pl
from jax.experimental.pallas import tpu as pltpu
from jax.sharding import PartitionSpec as P

MASKS = 512
SEGS = 128
LANES = 128
MIB = 2**20
VMEM = pl.BlockSpec(memory_space=pltpu.VMEM)
SMEM = pl.BlockSpec(memory_space=pltpu.SMEM)


class Sizes:
    def __init__(self, frame_count, band_height, det_cols):
        self.frames = frame_count
        self.rows = band_height
        self.cols = det_cols
        self.reach = band_height // 8
        self.ext = band_height + 2 * self.reach
        self.tiles = -(-det_cols // LANES)
        self.width = self.tiles * LANES
        self.pitch = frame_count + 1
        self.tall = -(-band_height // 16) * 16
        self.packed = 8 + -(-self.reach // 8) * 8


def widened(size, labels):
    fill = jnp.full((labels.shape[0], size.width - size.cols), -1.0, jnp.float32)
    return jnp.concatenate([labels.astype(jnp.float32), fill], axis=1)


def diagonal_kernel(size, out):
    place = lax.broadcasted_iota(jnp.int32, out.shape, 1)
    row = lax.broadcasted_iota(jnp.int32, out.shape, 0)
    chosen = (place == row) | (place == row + size.rows) | (place == row + 2 * size.rows)
    out[...] = jnp.where(chosen & (row < size.rows), 1.0, 0.0).astype(jnp.bfloat16)


def diagonals(size):
    return pl.pallas_call(
        functools.partial(diagonal_kernel, size),
        out_shape=jax.ShapeDtypeStruct((size.tall, 2 * LANES), jnp.bfloat16),
        out_specs=VMEM,
        compiler_params=pltpu.CompilerParams(vmem_limit_bytes=2 * MIB),
        cost_estimate=pl.CostEstimate(flops=10**10, bytes_accessed=10**6, transcendentals=0),
        name="diagonals",
    )()


def prepare_kernel(size, diagonal, scales, labels, moved, spread, wide, split):
    frames, rows = size.frames, size.rows
    empty = jnp.zeros((frames, LANES), jnp.float32)

    def clear(e, carry):
        for t in range(size.tiles):
            moved[t, pl.ds(e * size.pitch, frames), :] = empty
            moved[t, pl.ds((e + rows) * size.pitch, frames), :] = empty
        return carry

    lax.fori_loop(0, 2 * size.reach, clear, 0, unroll=3)

    whole = scales[...]
    high = whole.astype(jnp.bfloat16).astype(jnp.float32)
    middle = (whole - high).astype(jnp.bfloat16).astype(jnp.float32)
    rest = jnp.zeros((frames, 2 * LANES - rows), jnp.float32)
    parts = [
        pltpu.roll(jnp.concatenate([part, rest], axis=1), k * rows, 1)
        for k, part in enumerate([high, middle, whole - high - middle])
    ]
    split[...] = parts[0] + parts[1] + parts[2]
    tall = size.tall
    group = 8
    ones = jnp.ones((2 * LANES, LANES), jnp.bfloat16)

    def spread_group(i, carry):
        chosen = []
        for j in range(group):
            line = split[pl.ds(i * group + j, 1), :]
            line = jnp.broadcast_to(line, (16, 2 * LANES)).astype(jnp.bfloat16)
            chosen.append(jnp.concatenate([line] * (tall // 16), axis=0) * diagonal[...])
        at = pl.multiple_of(i * (group * tall), 8)
        spread[pl.ds(at, group * tall), :] = jnp.dot(
            jnp.concatenate(chosen, axis=0), ones, preferred_element_type=jnp.float32
        )
        return carry

    lax.fori_loop(0, frames // group, spread_group, 0, unroll=8)
    wide[...] = widened(size, labels[...])


def prepare(size, diagonal, scales, labels):
    return pl.pallas_call(
        functools.partial(prepare_kernel, size),
        out_shape=[
            jax.ShapeDtypeStruct((size.tiles, size.ext * size.pitch, LANES), jnp.float32),
            jax.ShapeDtypeStruct((size.frames * size.tall, LANES), jnp.float32),
            jax.ShapeDtypeStruct((size.rows, size.width), jnp.float32),
        ],
        in_specs=[VMEM] * 3,
        out_specs=[VMEM] * 3,
        scratch_shapes=[pltpu.VMEM((size.frames, 2 * LANES), jnp.float32)],
        compiler_params=pltpu.CompilerParams(vmem_limit_bytes=8 * MIB),
        cost_estimate=pl.CostEstimate(flops=5 * 10**8, bytes_accessed=10**6, transcendentals=0),
        name="prepare",
    )(diagonal, scales, labels)


def shift_kernel(size, row_shift, col_shift, spread, codes, wide, cleared, moved, payload, total):
    frames, rows, cols, tiles, reach = size.frames, size.rows, size.cols, size.tiles, size.reach
    total[...] = jnp.zeros((rows, LANES), jnp.float32)
    whole_lane = lax.broadcasted_iota(jnp.int32, (rows, LANES), 1)
    lane = whole_lane.astype(jnp.float32).astype(jnp.bfloat16)
    source = lax.broadcasted_iota(jnp.int32, (rows, LANES), 0)
    band = lax.axis_index("band")
    zero = jnp.zeros((rows, LANES), jnp.bfloat16)

    def shift_frame(f, carry):
        down, right = row_shift[f], col_shift[f]
        turn = jnp.where(right < 0, right + LANES, right)
        left_end = jnp.where(right < 0, 0, turn).astype(jnp.float32).astype(jnp.bfloat16)
        right_start = jnp.where(right < 0, turn, LANES).astype(jnp.float32).astype(jnp.bfloat16)
        from_left = lane < left_end
        from_right = lane >= right_start
        scale_f = spread[pl.ds(pl.multiple_of(f * size.tall, 8), rows), :]
        turned = [zero]
        for t in range(tiles):
            upper = min(cols, (t + 1) * LANES)
            value = codes[f, :, t * LANES : upper].astype(jnp.float32)
            if upper < (t + 1) * LANES:
                fill = jnp.zeros((rows, (t + 1) * LANES - upper), jnp.float32)
                value = jnp.concatenate([value, fill], axis=1)
            turned.append(pltpu.roll((value * scale_f).astype(jnp.bfloat16), turn, 1))
        turned.append(zero)
        start = (reach + down) * size.pitch + f
        row_sum = jnp.zeros((rows, LANES), jnp.float32)
        for t in range(tiles):
            out = jnp.where(
                from_left, turned[t], jnp.where(from_right, turned[t + 2], turned[t + 1])
            ).astype(jnp.float32)
            moved[t, pl.ds(start, rows, stride=size.pitch), :] = out
            if (t + 1) * LANES > cols:
                out = jnp.where(whole_lane < cols - t * LANES, out, 0.0)
            row_sum = row_sum + out
        target = source + (band * rows + down)
        total[...] += jnp.where((target >= 0) & (target < cols), row_sum, 0.0)
        return carry

    lax.fori_loop(0, frames, shift_frame, 0, unroll=4)
    payload[0:8, 0:LANES] = jnp.sum(total[...].reshape(rows // 8, 8, LANES), axis=0)
    top, bottom = wide[0:reach, :], wide[rows - reach : rows, :]
    payload[8 : 8 + reach, :] = jnp.where(band % 2 == 0, bottom, top)


def shift_frames(size, row_shift, col_shift, spread, codes, wide, cleared):
    return pl.pallas_call(
        functools.partial(shift_kernel, size),
        out_shape=[
            jax.ShapeDtypeStruct(cleared.shape, jnp.float32),
            jax.ShapeDtypeStruct((size.packed, size.width), jnp.float32),
        ],
        in_specs=[SMEM] * 2 + [VMEM] * 4,
        out_specs=[VMEM] * 2,
        scratch_shapes=[pltpu.VMEM((size.rows, LANES), jnp.float32)],
        input_output_aliases={5: 0},
        compiler_params=pltpu.CompilerParams(vmem_limit_bytes=12 * MIB),
        cost_estimate=pl.CostEstimate(flops=6 * 10**9, bytes_accessed=10**6, transcendentals=0),
        name="shift",
    )(row_shift, col_shift, spread, codes, wide, cleared)


def table_consts(size):
    segment = lax.broadcasted_iota(jnp.int32, (16, size.width), 0)
    column = lax.broadcasted_iota(jnp.int32, (16, size.width), 1).astype(jnp.float32)
    xcoord = ((column + 0.5) / size.cols - 0.5).astype(jnp.bfloat16)
    ids = [
        (segment + 16 * k).astype(jnp.float32).astype(jnp.bfloat16) for k in range(SEGS // 16)
    ]
    return ids, xcoord


def add_row(size, consts, label_row, values, moments, e):
    ids, xcoord = consts
    zero = jnp.zeros((16, size.width), jnp.bfloat16)
    one = jnp.ones((16, size.width), jnp.bfloat16)
    label = jnp.broadcast_to(label_row, (16, size.width)).astype(jnp.bfloat16)
    plain, by_x = [], []
    for k in range(SEGS // 16):
        same = label == ids[k]
        plain.append(jnp.where(same, one, zero))
        by_x.append(jnp.where(same, xcoord, zero))
    table = jnp.concatenate(plain + by_x, axis=0)
    sums = lax.dot_general(
        table, values, (((1,), (1,)), ((), ())), preferred_element_type=jnp.float32
    )
    first_row = lax.axis_index("band") * size.rows
    offset = (first_row + e - size.reach).astype(jnp.float32)
    ycoord = ((offset + 0.5) / size.cols - 0.5).astype(jnp.bfloat16).astype(jnp.float32)
    moments[0:SEGS, :] += sums[0:SEGS]
    moments[SEGS : 2 * SEGS, :] += sums[0:SEGS] * ycoord
    moments[2 * SEGS : 3 * SEGS, :] += sums[SEGS : 2 * SEGS]


def values_of(size, moved, e):
    base = e * size.pitch
    tiles = [
        moved[t, pl.ds(base, size.frames), :].astype(jnp.bfloat16) for t in range(size.tiles)
    ]
    return jnp.concatenate(tiles, axis=1)


def core_kernel(size, first, last, started, moved, wide, token, *refs):
    if started:
        before, moments = refs
        moments[...] = before[...]
    else:
        (moments,) = refs
        moments[...] = jnp.zeros(moments.shape, jnp.float32)
    consts = table_consts(size)

    def step(r, carry):
        e = r + size.reach
        add_row(size, consts, wide[pl.ds(r, 1), :], values_of(size, moved, e), moments, e)
        return carry

    lax.fori_loop(first, last, step, 0, unroll=9)


def core_rows(size, moved, wide, token, before, first, last):
    args = [moved, wide, token] + ([] if before is None else [before])
    specs = [VMEM, VMEM, pl.BlockSpec(memory_space=pl.ANY)] + [VMEM] * (len(args) - 3)
    return pl.pallas_call(
        functools.partial(core_kernel, size, first, last, before is not None),
        out_shape=jax.ShapeDtypeStruct((3 * SEGS, size.frames), jnp.float32),
        in_specs=specs,
        out_specs=VMEM,
        compiler_params=pltpu.CompilerParams(vmem_limit_bytes=8 * MIB),
        cost_estimate=pl.CostEstimate(flops=4 * 10**9, bytes_accessed=10**6, transcendentals=0),
        name="core",
    )(*args)


def edge_kernel(size, moved, first_got, second_got, token, before, coeffs, send, wide, moments):
    frames, rows, reach = size.frames, size.rows, size.reach
    moments[...] = before[...]
    band, bands = lax.axis_index("band"), lax.axis_size("band")
    even = band % 2 == 0
    first, second = first_got[8 : 8 + reach, :], second_got[8 : 8 + reach, :]
    wide[0:reach, :] = jnp.where(even, second, first)
    wide[reach : 2 * reach, :] = jnp.where(even, first, second)
    nothing = jnp.full((reach, size.width), -1.0, jnp.float32)

    @pl.when(band == 0)
    def _():
        wide[0:reach, :] = nothing

    @pl.when(band == bands - 1)
    def _():
        wide[reach : 2 * reach, :] = nothing

    consts = table_consts(size)

    def step(r, carry):
        e = jnp.where(r < reach, r, r + rows)
        add_row(size, consts, wide[pl.ds(r, 1), :], values_of(size, moved, e), moments, e)
        return carry

    lax.fori_loop(0, 2 * reach, step, 0, unroll=9)
    partial = jnp.dot(
        moments[...].T,
        coeffs[...],
        precision=lax.Precision.HIGHEST,
        preferred_element_type=jnp.float32,
    )
    half = frames // 2
    width = MASKS // bands
    per = LANES // width
    lane = lax.broadcasted_iota(jnp.int32, (half, LANES), 1)
    for b in range(bands):
        at = (b // per) * LANES
        low = partial[:half, at : at + LANES]
        high = partial[half:, at : at + LANES]
        if b % per == 0:
            high = pltpu.roll(high, width, 1)
        else:
            low = pltpu.roll(low, width, 1)
        send[b, 0:half, :] = jnp.where(lane < width, low, high)


def edge_rows(size, moved, first_got, second_got, token, before, coeffs):
    return pl.pallas_call(
        functools.partial(edge_kernel, size),
        out_shape=jax.ShapeDtypeStruct(
            (lax.axis_size("band"), size.frames // 2 + 8, LANES), jnp.float32
        ),
        in_specs=[VMEM, VMEM, VMEM, pl.BlockSpec(memory_space=pl.ANY), VMEM, VMEM],
        out_specs=VMEM,
        scratch_shapes=[
            pltpu.VMEM((2 * size.reach, size.width), jnp.float32),
            pltpu.VMEM((3 * SEGS, size.frames), jnp.float32),
        ],
        compiler_params=pltpu.CompilerParams(vmem_limit_bytes=12 * MIB),
        cost_estimate=pl.CostEstimate(flops=4 * 10**9, bytes_accessed=10**6, transcendentals=0),
        name="edge",
    )(moved, first_got, second_got, token, before, coeffs)


def join_kernel(size, own, other, wide, token, out):
    out[0:8, 0:LANES] = own[0:8, 0:LANES] + other[0:8, 0:LANES]
    if out.shape[0] > 8:
        top, bottom = wide[0 : size.reach, :], wide[size.rows - size.reach : size.rows, :]
        out[8 : 8 + size.reach, :] = jnp.where(lax.axis_index("band") % 2 == 0, top, bottom)


def join(size, own, other, wide, token, with_labels):
    shape = (size.packed, size.width) if with_labels else (8, LANES)
    return pl.pallas_call(
        functools.partial(join_kernel, size),
        out_shape=jax.ShapeDtypeStruct(shape, jnp.float32),
        in_specs=[VMEM, VMEM, VMEM, pl.BlockSpec(memory_space=pl.ANY)],
        out_specs=VMEM,
        compiler_params=pltpu.CompilerParams(vmem_limit_bytes=2 * MIB),
        name="join",
    )(own, other, wide, token)


def put_kernel(send, own, other, out):
    bands, height, _ = out.shape
    for b in range(bands):
        out[b, height - 8 : height, :] = own[0:8, 0:LANES] + other[0:8, 0:LANES]


def put_total(send, own, other):
    return pl.pallas_call(
        put_kernel,
        out_shape=jax.ShapeDtypeStruct(send.shape, jnp.float32),
        in_specs=[VMEM] * 3,
        out_specs=VMEM,
        input_output_aliases={0: 0},
        compiler_params=pltpu.CompilerParams(vmem_limit_bytes=2 * MIB),
        name="put",
    )(send, own, other)


def finish_kernel(frame_total, blocks, out):
    bands, height, _ = blocks.shape
    half = height - 8
    summed = blocks[0]
    for b in range(1, bands):
        summed = summed + blocks[b]
    mean_total = jnp.sum(summed[half:, :]) / frame_total
    scaled = summed[:half] / mean_total
    width = out.shape[1]
    out[0:half, :] = scaled[:, :width]
    out[half:, :] = scaled[:, width:]


def finish(blocks, frame_count):
    half = frame_count // 2
    return pl.pallas_call(
        functools.partial(finish_kernel, float(frame_count * lax.axis_size("scan"))),
        out_shape=jax.ShapeDtypeStruct((2 * half, LANES // 2), jnp.float32),
        in_specs=[VMEM],
        out_specs=VMEM,
        compiler_params=pltpu.CompilerParams(vmem_limit_bytes=8 * MIB),
        name="finish",
    )(blocks)


def partner_steps():
    scans, bands = lax.axis_size("scan"), lax.axis_size("band")
    around = {0: 3, 1: 2, 2: 1, 3: 0}

    def x_around(s):
        return (s // 8) * 8 + around[s // 2 % 4] * 2 + s % 2

    def z_around(s):
        return around[s // 8] * 8 + s % 8

    def same(b):
        return b

    def upper_pair(b):
        return b ^ 1

    def lower_pair(b):
        return (((b + 1) % bands) ^ 1) - 1 if ((b + 1) % bands) ^ 1 else bands - 1

    moves = [
        (lambda s: s ^ 1, upper_pair),
        (lambda s: s ^ 2, lower_pair),
        (x_around, same),
        (lambda s: s ^ 8, same),
        (z_around, same),
    ]
    return [
        [(s * bands + b, move(s) * bands + turn(b)) for s in range(scans) for b in range(bands)]
        for move, turn in moves
    ]


def body(frame_codes, row_scales, row_shift, col_shift, segment_labels, mask_coeffs):
    frame_count, band_height, det_cols = frame_codes.shape
    size = Sizes(frame_count, band_height, det_cols)
    cleared, spread, wide = prepare(size, diagonals(size), row_scales, segment_labels)
    moved, total = shift_frames(size, row_shift, col_shift, spread, frame_codes, wide, cleared)
    coeffs = mask_coeffs.reshape(3 * SEGS, MASKS)
    steps = partner_steps()
    cuts = [band_height * i // (len(steps) - 1) for i in range(len(steps))]
    moments, got = None, []
    for i, pairs in enumerate(steps):
        got.append(lax.ppermute(total, ("scan", "band"), pairs))
        if i < len(steps) - 1:
            moments = core_rows(size, moved, wide, total, moments, cuts[i], cuts[i + 1])
            total = join(size, total, got[i], wide, moments, i == 0)
    send = edge_rows(size, moved, got[0], got[1], total, moments, coeffs)
    send = put_total(send, total, got[-1])
    blocks = lax.all_to_all(send, "band", 0, 0)
    return finish(blocks, frame_count)


def solution(mesh):
    return jax.shard_map(
        body,
        mesh=mesh,
        in_specs=(
            P("scan", "band", None),
            P("scan", "band"),
            P("scan"),
            P("scan"),
            P("band", None),
            P(),
        ),
        out_specs=P("scan", "band"),
        check_vma=False,
    )
```

```python
import functools

import jax
import jax.numpy as jnp
from jax import lax
from jax.experimental import pallas as pl
from jax.experimental.pallas import tpu as pltpu
from jax.sharding import PartitionSpec as P

MASKS = 512
SEGS = 128
LANES = 128
MIB = 2**20
VMEM = pl.BlockSpec(memory_space=pltpu.VMEM)
SMEM = pl.BlockSpec(memory_space=pltpu.SMEM)


class Sizes:
    def __init__(self, frame_count, band_height, det_cols):
        self.frames = frame_count
        self.rows = band_height
        self.cols = det_cols
        self.reach = band_height // 8
        self.ext = band_height + 2 * self.reach
        self.tiles = -(-det_cols // LANES)
        self.width = self.tiles * LANES
        self.pitch = frame_count + 1
        self.tall = -(-band_height // 16) * 16
        self.packed = -(-(self.reach + 3) // 16) * 16


def widened(size, labels):
    fill = jnp.full((labels.shape[0], size.width - size.cols), -1.0, jnp.float32)
    return jnp.concatenate([labels.astype(jnp.float32), fill], axis=1)


def diagonal_kernel(size, out):
    place = lax.broadcasted_iota(jnp.int32, out.shape, 1)
    row = lax.broadcasted_iota(jnp.int32, out.shape, 0)
    chosen = (place == row) | (place == row + size.rows) | (place == row + 2 * size.rows)
    out[...] = jnp.where(chosen & (row < size.rows), 1.0, 0.0).astype(jnp.bfloat16)


def diagonals(size):
    return pl.pallas_call(
        functools.partial(diagonal_kernel, size),
        out_shape=jax.ShapeDtypeStruct((size.tall, 2 * LANES), jnp.bfloat16),
        out_specs=VMEM,
        compiler_params=pltpu.CompilerParams(vmem_limit_bytes=2 * MIB),
        cost_estimate=pl.CostEstimate(flops=10**10, bytes_accessed=10**6, transcendentals=0),
        name="diagonals",
    )()


def prepare_kernel(size, diagonal, scales, labels, moved, spread, wide, split):
    frames, rows = size.frames, size.rows
    empty = jnp.zeros((frames, LANES), jnp.float32)

    def clear(e, carry):
        for t in range(size.tiles):
            moved[t, pl.ds(e * size.pitch, frames), :] = empty
            moved[t, pl.ds((e + rows) * size.pitch, frames), :] = empty
        return carry

    lax.fori_loop(0, 2 * size.reach, clear, 0, unroll=3)

    whole = scales[...]
    high = whole.astype(jnp.bfloat16).astype(jnp.float32)
    middle = (whole - high).astype(jnp.bfloat16).astype(jnp.float32)
    rest = jnp.zeros((frames, 2 * LANES - rows), jnp.float32)
    parts = [
        pltpu.roll(jnp.concatenate([part, rest], axis=1), k * rows, 1)
        for k, part in enumerate([high, middle, whole - high - middle])
    ]
    split[...] = parts[0] + parts[1] + parts[2]
    tall = size.tall
    group = 8
    ones = jnp.ones((2 * LANES, LANES), jnp.bfloat16)

    def spread_group(i, carry):
        chosen = []
        for j in range(group):
            line = split[pl.ds(i * group + j, 1), :]
            line = jnp.broadcast_to(line, (16, 2 * LANES)).astype(jnp.bfloat16)
            chosen.append(jnp.concatenate([line] * (tall // 16), axis=0) * diagonal[...])
        at = pl.multiple_of(i * (group * tall), 8)
        spread[pl.ds(at, group * tall), :] = jnp.dot(
            jnp.concatenate(chosen, axis=0), ones, preferred_element_type=jnp.float32
        )
        return carry

    lax.fori_loop(0, frames // group, spread_group, 0, unroll=8)
    wide[...] = widened(size, labels[...])


def prepare(size, diagonal, scales, labels):
    return pl.pallas_call(
        functools.partial(prepare_kernel, size),
        out_shape=[
            jax.ShapeDtypeStruct((size.tiles, size.ext * size.pitch, LANES), jnp.float32),
            jax.ShapeDtypeStruct((size.frames * size.tall, LANES), jnp.float32),
            jax.ShapeDtypeStruct((size.rows, size.width), jnp.float32),
        ],
        in_specs=[VMEM] * 3,
        out_specs=[VMEM] * 3,
        scratch_shapes=[pltpu.VMEM((size.frames, 2 * LANES), jnp.float32)],
        compiler_params=pltpu.CompilerParams(vmem_limit_bytes=8 * MIB),
        cost_estimate=pl.CostEstimate(flops=5 * 10**8, bytes_accessed=10**6, transcendentals=0),
        name="prepare",
    )(diagonal, scales, labels)


def pack(size, out, lines, labels, sums):
    high = sums.astype(jnp.bfloat16).astype(jnp.float32)
    middle = (sums - high).astype(jnp.bfloat16).astype(jnp.float32)
    lines[...] = jnp.zeros(lines.shape, jnp.float32)
    lines[0 : size.reach, :] = labels
    for k, part in enumerate([high, middle, sums - high - middle]):
        lines[size.reach + k : size.reach + k + 1, 0:LANES] = part
    out[...] = lines[...].astype(jnp.bfloat16)


def packed_sums(size, message):
    parts = message[...].astype(jnp.float32)[size.reach : size.reach + 3, 0:LANES]
    return parts[0:1] + parts[1:2] + parts[2:3]


def shift_kernel(
    size, row_shift, col_shift, spread, codes, wide, cleared, moved, payload, total, lines
):
    frames, rows, cols, tiles, reach = size.frames, size.rows, size.cols, size.tiles, size.reach
    total[...] = jnp.zeros((rows, LANES), jnp.float32)
    whole_lane = lax.broadcasted_iota(jnp.int32, (rows, LANES), 1)
    lane = whole_lane.astype(jnp.float32).astype(jnp.bfloat16)
    source = lax.broadcasted_iota(jnp.int32, (rows, LANES), 0)
    band = lax.axis_index("band")
    zero = jnp.zeros((rows, LANES), jnp.bfloat16)

    def shift_frame(f, carry):
        down, right = row_shift[f], col_shift[f]
        turn = jnp.where(right < 0, right + LANES, right)
        left_end = jnp.where(right < 0, 0, turn).astype(jnp.float32).astype(jnp.bfloat16)
        right_start = jnp.where(right < 0, turn, LANES).astype(jnp.float32).astype(jnp.bfloat16)
        from_left = lane < left_end
        from_right = lane >= right_start
        scale_f = spread[pl.ds(pl.multiple_of(f * size.tall, 8), rows), :]
        turned = [zero]
        for t in range(tiles):
            upper = min(cols, (t + 1) * LANES)
            value = codes[f, :, t * LANES : upper].astype(jnp.float32)
            if upper < (t + 1) * LANES:
                fill = jnp.zeros((rows, (t + 1) * LANES - upper), jnp.float32)
                value = jnp.concatenate([value, fill], axis=1)
            turned.append(pltpu.roll((value * scale_f).astype(jnp.bfloat16), turn, 1))
        turned.append(zero)
        start = (reach + down) * size.pitch + f
        row_sum = jnp.zeros((rows, LANES), jnp.float32)
        for t in range(tiles):
            out = jnp.where(
                from_left, turned[t], jnp.where(from_right, turned[t + 2], turned[t + 1])
            ).astype(jnp.float32)
            moved[t, pl.ds(start, rows, stride=size.pitch), :] = out
            if (t + 1) * LANES > cols:
                out = jnp.where(whole_lane < cols - t * LANES, out, 0.0)
            row_sum = row_sum + out
        target = source + (band * rows + down)
        total[...] += jnp.where((target >= 0) & (target < cols), row_sum, 0.0)
        return carry

    lax.fori_loop(0, frames, shift_frame, 0, unroll=4)
    top, bottom = wide[0:reach, :], wide[rows - reach : rows, :]
    labels = jnp.where(band % 2 == 1, bottom, top)
    pack(size, payload, lines, labels, jnp.sum(total[...], axis=0, keepdims=True))


def shift_frames(size, row_shift, col_shift, spread, codes, wide, cleared):
    return pl.pallas_call(
        functools.partial(shift_kernel, size),
        out_shape=[
            jax.ShapeDtypeStruct(cleared.shape, jnp.float32),
            jax.ShapeDtypeStruct((size.packed, size.width), jnp.bfloat16),
        ],
        in_specs=[SMEM] * 2 + [VMEM] * 4,
        out_specs=[VMEM] * 2,
        scratch_shapes=[
            pltpu.VMEM((size.rows, LANES), jnp.float32),
            pltpu.VMEM((size.packed, size.width), jnp.float32),
        ],
        input_output_aliases={5: 0},
        compiler_params=pltpu.CompilerParams(vmem_limit_bytes=12 * MIB),
        cost_estimate=pl.CostEstimate(flops=6 * 10**9, bytes_accessed=10**6, transcendentals=0),
        name="shift",
    )(row_shift, col_shift, spread, codes, wide, cleared)


def table_consts(size):
    segment = lax.broadcasted_iota(jnp.int32, (16, size.width), 0)
    column = lax.broadcasted_iota(jnp.int32, (16, size.width), 1).astype(jnp.float32)
    xcoord = ((column + 0.5) / size.cols - 0.5).astype(jnp.bfloat16)
    ids = [
        (segment + 16 * k).astype(jnp.float32).astype(jnp.bfloat16) for k in range(SEGS // 16)
    ]
    return ids, xcoord


def add_row(size, consts, label_row, values, moments, e):
    ids, xcoord = consts
    zero = jnp.zeros((16, size.width), jnp.bfloat16)
    one = jnp.ones((16, size.width), jnp.bfloat16)
    label = jnp.broadcast_to(label_row, (16, size.width)).astype(jnp.bfloat16)
    plain, by_x = [], []
    for k in range(SEGS // 16):
        same = label == ids[k]
        plain.append(jnp.where(same, one, zero))
        by_x.append(jnp.where(same, xcoord, zero))
    table = jnp.concatenate(plain + by_x, axis=0)
    sums = lax.dot_general(
        table, values, (((1,), (1,)), ((), ())), preferred_element_type=jnp.float32
    )
    first_row = lax.axis_index("band") * size.rows
    offset = (first_row + e - size.reach).astype(jnp.float32)
    ycoord = ((offset + 0.5) / size.cols - 0.5).astype(jnp.bfloat16).astype(jnp.float32)
    moments[0:SEGS, :] += sums[0:SEGS]
    moments[SEGS : 2 * SEGS, :] += sums[0:SEGS] * ycoord
    moments[2 * SEGS : 3 * SEGS, :] += sums[SEGS : 2 * SEGS]


def values_of(size, moved, e):
    base = e * size.pitch
    tiles = [
        moved[t, pl.ds(base, size.frames), :].astype(jnp.bfloat16) for t in range(size.tiles)
    ]
    return jnp.concatenate(tiles, axis=1)


def core_kernel(size, first, last, started, moved, wide, token, *refs):
    if started:
        before, moments = refs
        moments[...] = before[...]
    else:
        (moments,) = refs
        moments[...] = jnp.zeros(moments.shape, jnp.float32)
    consts = table_consts(size)

    def step(r, carry):
        e = r + size.reach
        add_row(size, consts, wide[pl.ds(r, 1), :], values_of(size, moved, e), moments, e)
        return carry

    lax.fori_loop(first, last, step, 0, unroll=9)


def core_rows(size, moved, wide, token, before, first, last):
    args = [moved, wide, token] + ([] if before is None else [before])
    specs = [VMEM, VMEM, pl.BlockSpec(memory_space=pl.ANY)] + [VMEM] * (len(args) - 3)
    return pl.pallas_call(
        functools.partial(core_kernel, size, first, last, before is not None),
        out_shape=jax.ShapeDtypeStruct((3 * SEGS, size.frames), jnp.float32),
        in_specs=specs,
        out_specs=VMEM,
        compiler_params=pltpu.CompilerParams(vmem_limit_bytes=8 * MIB),
        cost_estimate=pl.CostEstimate(flops=4 * 10**9, bytes_accessed=10**6, transcendentals=0),
        name="core",
    )(*args)


def edge_kernel(size, moved, first_got, second_got, token, before, coeffs, send, wide, moments):
    frames, rows, reach = size.frames, size.rows, size.reach
    moments[...] = before[...]
    band, bands = lax.axis_index("band"), lax.axis_size("band")
    odd = band % 2 == 1
    first = first_got[...].astype(jnp.float32)[0:reach, :]
    second = second_got[...].astype(jnp.float32)[0:reach, :]
    wide[0:reach, :] = jnp.where(odd, second, first)
    wide[reach : 2 * reach, :] = jnp.where(odd, first, second)
    nothing = jnp.full((reach, size.width), -1.0, jnp.float32)

    @pl.when(band == 0)
    def _():
        wide[0:reach, :] = nothing

    @pl.when(band == bands - 1)
    def _():
        wide[reach : 2 * reach, :] = nothing

    consts = table_consts(size)

    def step(r, carry):
        e = jnp.where(r < reach, r, r + rows)
        add_row(size, consts, wide[pl.ds(r, 1), :], values_of(size, moved, e), moments, e)
        return carry

    lax.fori_loop(0, 2 * reach, step, 0, unroll=9)
    partial = jnp.dot(
        moments[...].T,
        coeffs[...],
        precision=lax.Precision.HIGHEST,
        preferred_element_type=jnp.float32,
    )
    half = frames // 2
    width = MASKS // bands
    per = LANES // width
    lane = lax.broadcasted_iota(jnp.int32, (half, LANES), 1)
    for b in range(bands):
        at = (b // per) * LANES
        low = partial[:half, at : at + LANES]
        high = partial[half:, at : at + LANES]
        if b % per == 0:
            high = pltpu.roll(high, width, 1)
        else:
            low = pltpu.roll(low, width, 1)
        send[b, 0:half, :] = jnp.where(lane < width, low, high)


def edge_rows(size, moved, first_got, second_got, token, before, coeffs):
    return pl.pallas_call(
        functools.partial(edge_kernel, size),
        out_shape=jax.ShapeDtypeStruct(
            (lax.axis_size("band"), size.frames // 2 + 8, LANES), jnp.float32
        ),
        in_specs=[VMEM, VMEM, VMEM, pl.BlockSpec(memory_space=pl.ANY), VMEM, VMEM],
        out_specs=VMEM,
        scratch_shapes=[
            pltpu.VMEM((2 * size.reach, size.width), jnp.float32),
            pltpu.VMEM((3 * SEGS, size.frames), jnp.float32),
        ],
        compiler_params=pltpu.CompilerParams(vmem_limit_bytes=12 * MIB),
        cost_estimate=pl.CostEstimate(flops=4 * 10**9, bytes_accessed=10**6, transcendentals=0),
        name="edge",
    )(moved, first_got, second_got, token, before, coeffs)


def first_join_kernel(size, own, other, wide, token, out, lines):
    top, bottom = wide[0 : size.reach, :], wide[size.rows - size.reach : size.rows, :]
    labels = jnp.where(lax.axis_index("band") % 2 == 1, top, bottom)
    pack(size, out, lines, labels, packed_sums(size, own) + packed_sums(size, other))


def second_join_kernel(size, own, other, wide, token, out, lines):
    out[...] = jnp.zeros(out.shape, jnp.float32)
    out[0:1, :] = packed_sums(size, own) + packed_sums(size, other)


def join_kernel(size, own, other, wide, token, out, lines):
    out[...] = own[...] + other[...]


def join(size, kernel, own, other, wide, token):
    out = jax.ShapeDtypeStruct((8, LANES), jnp.float32)
    if kernel is first_join_kernel:
        out = jax.ShapeDtypeStruct(own.shape, own.dtype)
    return pl.pallas_call(
        functools.partial(kernel, size),
        out_shape=out,
        in_specs=[VMEM, VMEM, VMEM, pl.BlockSpec(memory_space=pl.ANY)],
        out_specs=VMEM,
        scratch_shapes=[pltpu.VMEM((size.packed, size.width), jnp.float32)],
        compiler_params=pltpu.CompilerParams(vmem_limit_bytes=2 * MIB),
        name="join",
    )(own, other, wide, token)


def put_kernel(send, own, other, out):
    bands, height, _ = out.shape
    for b in range(bands):
        out[b, height - 8 : height, :] = own[...] + other[...]


def put_total(send, own, other):
    return pl.pallas_call(
        put_kernel,
        out_shape=jax.ShapeDtypeStruct(send.shape, jnp.float32),
        in_specs=[VMEM] * 3,
        out_specs=VMEM,
        input_output_aliases={0: 0},
        compiler_params=pltpu.CompilerParams(vmem_limit_bytes=2 * MIB),
        name="put",
    )(send, own, other)


def finish_kernel(frame_total, blocks, out):
    bands, height, _ = blocks.shape
    half = height - 8
    summed = blocks[0]
    for b in range(1, bands):
        summed = summed + blocks[b]
    mean_total = jnp.sum(summed[half:, :]) / frame_total
    scaled = summed[:half] / mean_total
    width = out.shape[1]
    out[0:half, :] = scaled[:, :width]
    out[half:, :] = scaled[:, width:]


def finish(blocks, frame_count):
    half = frame_count // 2
    return pl.pallas_call(
        functools.partial(finish_kernel, float(frame_count * lax.axis_size("scan"))),
        out_shape=jax.ShapeDtypeStruct((2 * half, LANES // 2), jnp.float32),
        in_specs=[VMEM],
        out_specs=VMEM,
        compiler_params=pltpu.CompilerParams(vmem_limit_bytes=8 * MIB),
        name="finish",
    )(blocks)


def partner_steps():
    scans, bands = lax.axis_size("scan"), lax.axis_size("band")
    around = {0: 3, 1: 2, 2: 1, 3: 0}

    def x_around(s):
        return (s // 8) * 8 + around[s // 2 % 4] * 2 + s % 2

    def z_around(s):
        return around[s // 8] * 8 + s % 8

    def same(b):
        return b

    def upper_pair(b):
        return b ^ 1

    def lower_pair(b):
        return b if b in (0, bands - 1) else ((b + 1) ^ 1) - 1

    moves = [
        (lambda s: s ^ 1, lower_pair),
        (x_around, upper_pair),
        (lambda s: s ^ 8, same),
        (z_around, same),
        (lambda s: s ^ 2, same),
    ]
    return [
        [(s * bands + b, move(s) * bands + turn(b)) for s in range(scans) for b in range(bands)]
        for move, turn in moves
    ]


def body(frame_codes, row_scales, row_shift, col_shift, segment_labels, mask_coeffs):
    frame_count, band_height, det_cols = frame_codes.shape
    size = Sizes(frame_count, band_height, det_cols)
    cleared, spread, wide = prepare(size, diagonals(size), row_scales, segment_labels)
    moved, total = shift_frames(size, row_shift, col_shift, spread, frame_codes, wide, cleared)
    coeffs = mask_coeffs.reshape(3 * SEGS, MASKS)
    steps = partner_steps()
    cuts = [band_height * i // (len(steps) - 1) for i in range(len(steps))]
    joins = [first_join_kernel, second_join_kernel, join_kernel, join_kernel]
    moments, got = None, []
    for i, pairs in enumerate(steps):
        got.append(lax.ppermute(total, ("scan", "band"), pairs))
        if i < len(steps) - 1:
            moments = core_rows(size, moved, wide, total, moments, cuts[i], cuts[i + 1])
            total = join(size, joins[i], total, got[i], wide, moments)
    send = edge_rows(size, moved, got[0], got[1], total, moments, coeffs)
    send = put_total(send, total, got[-1])
    blocks = lax.all_to_all(send, "band", 0, 0)
    return finish(blocks, frame_count)


def solution(mesh):
    return jax.shard_map(
        body,
        mesh=mesh,
        in_specs=(
            P("scan", "band", None),
            P("scan", "band"),
            P("scan"),
            P("scan"),
            P("band", None),
            P(),
        ),
        out_specs=P("scan", "band"),
        check_vma=False,
    )
```

```python
import functools

import jax
import jax.numpy as jnp
from jax import lax
from jax.experimental import pallas as pl
from jax.experimental.pallas import tpu as pltpu
from jax.sharding import PartitionSpec as P

MASKS = 512
SEGS = 128
LANES = 128
MIB = 2**20
VMEM = pl.BlockSpec(memory_space=pltpu.VMEM)
SMEM = pl.BlockSpec(memory_space=pltpu.SMEM)


class Sizes:
    def __init__(self, frame_count, band_height, det_cols):
        self.frames = frame_count
        self.rows = band_height
        self.cols = det_cols
        self.reach = band_height // 8
        self.ext = band_height + 2 * self.reach
        self.tiles = -(-det_cols // LANES)
        self.width = self.tiles * LANES
        self.pitch = frame_count + 1
        self.tall = -(-band_height // 16) * 16
        self.packed = -(-(self.reach + 3) // 16) * 16


def widened(size, labels):
    fill = jnp.full((labels.shape[0], size.width - size.cols), -1.0, jnp.float32)
    return jnp.concatenate([labels.astype(jnp.float32), fill], axis=1)


def diagonal_kernel(size, out):
    place = lax.broadcasted_iota(jnp.int32, out.shape, 1)
    row = lax.broadcasted_iota(jnp.int32, out.shape, 0)
    chosen = (place == row) | (place == row + size.rows) | (place == row + 2 * size.rows)
    out[...] = jnp.where(chosen & (row < size.rows), 1.0, 0.0).astype(jnp.bfloat16)


def diagonals(size):
    return pl.pallas_call(
        functools.partial(diagonal_kernel, size),
        out_shape=jax.ShapeDtypeStruct((size.tall, 2 * LANES), jnp.bfloat16),
        out_specs=VMEM,
        compiler_params=pltpu.CompilerParams(vmem_limit_bytes=2 * MIB),
        cost_estimate=pl.CostEstimate(flops=10**10, bytes_accessed=10**6, transcendentals=0),
        name="diagonals",
    )()


def prepare_kernel(size, diagonal, scales, labels, moved, spread, wide, split):
    frames, rows = size.frames, size.rows
    empty = jnp.zeros((frames, LANES), jnp.float32)

    def clear(e, carry):
        for t in range(size.tiles):
            moved[t, pl.ds(e * size.pitch, frames), :] = empty
            moved[t, pl.ds((e + rows) * size.pitch, frames), :] = empty
        return carry

    lax.fori_loop(0, 2 * size.reach, clear, 0, unroll=3)

    whole = scales[...]
    high = whole.astype(jnp.bfloat16).astype(jnp.float32)
    middle = (whole - high).astype(jnp.bfloat16).astype(jnp.float32)
    rest = jnp.zeros((frames, 2 * LANES - rows), jnp.float32)
    parts = [
        pltpu.roll(jnp.concatenate([part, rest], axis=1), k * rows, 1)
        for k, part in enumerate([high, middle, whole - high - middle])
    ]
    split[...] = parts[0] + parts[1] + parts[2]
    tall = size.tall
    group = 8
    ones = jnp.ones((2 * LANES, LANES), jnp.bfloat16)

    def spread_group(i, carry):
        chosen = []
        for j in range(group):
            line = split[pl.ds(i * group + j, 1), :]
            line = jnp.broadcast_to(line, (16, 2 * LANES)).astype(jnp.bfloat16)
            chosen.append(jnp.concatenate([line] * (tall // 16), axis=0) * diagonal[...])
        at = pl.multiple_of(i * (group * tall), 8)
        spread[pl.ds(at, group * tall), :] = jnp.dot(
            jnp.concatenate(chosen, axis=0), ones, preferred_element_type=jnp.float32
        )
        return carry

    lax.fori_loop(0, frames // group, spread_group, 0, unroll=8)
    wide[...] = widened(size, labels[...])


def prepare(size, diagonal, scales, labels):
    return pl.pallas_call(
        functools.partial(prepare_kernel, size),
        out_shape=[
            jax.ShapeDtypeStruct((size.tiles, size.ext * size.pitch, LANES), jnp.float32),
            jax.ShapeDtypeStruct((size.frames * size.tall, LANES), jnp.float32),
            jax.ShapeDtypeStruct((size.rows, size.width), jnp.float32),
        ],
        in_specs=[VMEM] * 3,
        out_specs=[VMEM] * 3,
        scratch_shapes=[pltpu.VMEM((size.frames, 2 * LANES), jnp.float32)],
        compiler_params=pltpu.CompilerParams(vmem_limit_bytes=8 * MIB),
        cost_estimate=pl.CostEstimate(flops=5 * 10**8, bytes_accessed=10**6, transcendentals=0),
        name="prepare",
    )(diagonal, scales, labels)


def pack(size, out, lines, labels, sums):
    high = sums.astype(jnp.bfloat16).astype(jnp.float32)
    middle = (sums - high).astype(jnp.bfloat16).astype(jnp.float32)
    lines[...] = jnp.zeros(lines.shape, jnp.float32)
    lines[0 : size.reach, :] = labels
    for k, part in enumerate([high, middle, sums - high - middle]):
        lines[size.reach + k : size.reach + k + 1, 0:LANES] = part
    out[...] = lines[...].astype(jnp.bfloat16)


def packed_sums(size, message):
    parts = message[...].astype(jnp.float32)[size.reach : size.reach + 3, 0:LANES]
    return parts[0:1] + parts[1:2] + parts[2:3]


def shift_kernel(
    size, row_shift, col_shift, spread, codes, wide, cleared, moved, payload, labels_only, total, lines
):
    frames, rows, cols, tiles, reach = size.frames, size.rows, size.cols, size.tiles, size.reach
    total[...] = jnp.zeros((rows, LANES), jnp.float32)
    whole_lane = lax.broadcasted_iota(jnp.int32, (rows, LANES), 1)
    lane = whole_lane.astype(jnp.float32).astype(jnp.bfloat16)
    source = lax.broadcasted_iota(jnp.int32, (rows, LANES), 0)
    band = lax.axis_index("band")
    zero = jnp.zeros((rows, LANES), jnp.bfloat16)

    def shift_frame(f, carry):
        down, right = row_shift[f], col_shift[f]
        turn = jnp.where(right < 0, right + LANES, right)
        left_end = jnp.where(right < 0, 0, turn).astype(jnp.float32).astype(jnp.bfloat16)
        right_start = jnp.where(right < 0, turn, LANES).astype(jnp.float32).astype(jnp.bfloat16)
        from_left = lane < left_end
        from_right = lane >= right_start
        scale_f = spread[pl.ds(pl.multiple_of(f * size.tall, 8), rows), :]
        turned = [zero]
        for t in range(tiles):
            upper = min(cols, (t + 1) * LANES)
            value = codes[f, :, t * LANES : upper].astype(jnp.float32)
            if upper < (t + 1) * LANES:
                fill = jnp.zeros((rows, (t + 1) * LANES - upper), jnp.float32)
                value = jnp.concatenate([value, fill], axis=1)
            turned.append(pltpu.roll((value * scale_f).astype(jnp.bfloat16), turn, 1))
        turned.append(zero)
        start = (reach + down) * size.pitch + f
        row_sum = jnp.zeros((rows, LANES), jnp.float32)
        for t in range(tiles):
            out = jnp.where(
                from_left, turned[t], jnp.where(from_right, turned[t + 2], turned[t + 1])
            ).astype(jnp.float32)
            moved[t, pl.ds(start, rows, stride=size.pitch), :] = out
            if (t + 1) * LANES > cols:
                out = jnp.where(whole_lane < cols - t * LANES, out, 0.0)
            row_sum = row_sum + out
        target = source + (band * rows + down)
        total[...] += jnp.where((target >= 0) & (target < cols), row_sum, 0.0)
        return carry

    lax.fori_loop(0, frames, shift_frame, 0, unroll=4)
    top, bottom = wide[0:reach, :], wide[rows - reach : rows, :]
    pack(size, labels_only, lines, jnp.where(band % 2 == 1, top, bottom), jnp.zeros((1, LANES)))
    sums = jnp.sum(total[...], axis=0, keepdims=True)
    pack(size, payload, lines, jnp.where(band % 2 == 1, bottom, top), sums)


def shift_frames(size, row_shift, col_shift, spread, codes, wide, cleared):
    return pl.pallas_call(
        functools.partial(shift_kernel, size),
        out_shape=[
            jax.ShapeDtypeStruct(cleared.shape, jnp.float32),
            jax.ShapeDtypeStruct((size.packed, size.width), jnp.bfloat16),
            jax.ShapeDtypeStruct((size.packed, size.width), jnp.bfloat16),
        ],
        in_specs=[SMEM] * 2 + [VMEM] * 4,
        out_specs=[VMEM] * 3,
        scratch_shapes=[
            pltpu.VMEM((size.rows, LANES), jnp.float32),
            pltpu.VMEM((size.packed, size.width), jnp.float32),
        ],
        input_output_aliases={5: 0},
        compiler_params=pltpu.CompilerParams(vmem_limit_bytes=12 * MIB),
        cost_estimate=pl.CostEstimate(flops=6 * 10**9, bytes_accessed=10**6, transcendentals=0),
        name="shift",
    )(row_shift, col_shift, spread, codes, wide, cleared)


def table_consts(size):
    segment = lax.broadcasted_iota(jnp.int32, (16, size.width), 0)
    column = lax.broadcasted_iota(jnp.int32, (16, size.width), 1).astype(jnp.float32)
    xcoord = ((column + 0.5) / size.cols - 0.5).astype(jnp.bfloat16)
    ids = [
        (segment + 16 * k).astype(jnp.float32).astype(jnp.bfloat16) for k in range(SEGS // 16)
    ]
    return ids, xcoord


def add_row(size, consts, label_row, values, moments, e):
    ids, xcoord = consts
    zero = jnp.zeros((16, size.width), jnp.bfloat16)
    one = jnp.ones((16, size.width), jnp.bfloat16)
    label = jnp.broadcast_to(label_row, (16, size.width)).astype(jnp.bfloat16)
    plain, by_x = [], []
    for k in range(SEGS // 16):
        same = label == ids[k]
        plain.append(jnp.where(same, one, zero))
        by_x.append(jnp.where(same, xcoord, zero))
    table = jnp.concatenate(plain + by_x, axis=0)
    sums = lax.dot_general(
        table, values, (((1,), (1,)), ((), ())), preferred_element_type=jnp.float32
    )
    first_row = lax.axis_index("band") * size.rows
    offset = (first_row + e - size.reach).astype(jnp.float32)
    ycoord = ((offset + 0.5) / size.cols - 0.5).astype(jnp.bfloat16).astype(jnp.float32)
    moments[0:SEGS, :] += sums[0:SEGS]
    moments[SEGS : 2 * SEGS, :] += sums[0:SEGS] * ycoord
    moments[2 * SEGS : 3 * SEGS, :] += sums[SEGS : 2 * SEGS]


def values_of(size, moved, e):
    base = e * size.pitch
    tiles = [
        moved[t, pl.ds(base, size.frames), :].astype(jnp.bfloat16) for t in range(size.tiles)
    ]
    return jnp.concatenate(tiles, axis=1)


def core_kernel(size, first, last, started, moved, wide, token, *refs):
    if started:
        before, moments = refs
        moments[...] = before[...]
    else:
        (moments,) = refs
        moments[...] = jnp.zeros(moments.shape, jnp.float32)
    consts = table_consts(size)

    def step(r, carry):
        e = r + size.reach
        add_row(size, consts, wide[pl.ds(r, 1), :], values_of(size, moved, e), moments, e)
        return carry

    lax.fori_loop(first, last, step, 0, unroll=9)


def core_rows(size, moved, wide, token, before, first, last):
    args = [moved, wide, token] + ([] if before is None else [before])
    specs = [VMEM, VMEM, pl.BlockSpec(memory_space=pl.ANY)] + [VMEM] * (len(args) - 3)
    return pl.pallas_call(
        functools.partial(core_kernel, size, first, last, before is not None),
        out_shape=jax.ShapeDtypeStruct((3 * SEGS, size.frames), jnp.float32),
        in_specs=specs,
        out_specs=VMEM,
        compiler_params=pltpu.CompilerParams(vmem_limit_bytes=8 * MIB),
        cost_estimate=pl.CostEstimate(flops=4 * 10**9, bytes_accessed=10**6, transcendentals=0),
        name="core",
    )(*args)


def edge_kernel(size, moved, first_got, second_got, token, before, coeffs, send, wide, moments):
    frames, rows, reach = size.frames, size.rows, size.reach
    moments[...] = before[...]
    band, bands = lax.axis_index("band"), lax.axis_size("band")
    odd = band % 2 == 1
    first = first_got[...].astype(jnp.float32)[0:reach, :]
    second = second_got[...].astype(jnp.float32)[0:reach, :]
    wide[0:reach, :] = jnp.where(odd, second, first)
    wide[reach : 2 * reach, :] = jnp.where(odd, first, second)
    nothing = jnp.full((reach, size.width), -1.0, jnp.float32)

    @pl.when(band == 0)
    def _():
        wide[0:reach, :] = nothing

    @pl.when(band == bands - 1)
    def _():
        wide[reach : 2 * reach, :] = nothing

    consts = table_consts(size)

    def step(r, carry):
        e = jnp.where(r < reach, r, r + rows)
        add_row(size, consts, wide[pl.ds(r, 1), :], values_of(size, moved, e), moments, e)
        return carry

    lax.fori_loop(0, 2 * reach, step, 0, unroll=9)
    partial = jnp.dot(
        moments[...].T,
        coeffs[...],
        precision=lax.Precision.HIGHEST,
        preferred_element_type=jnp.float32,
    )
    half = frames // 2
    width = MASKS // bands
    per = LANES // width
    lane = lax.broadcasted_iota(jnp.int32, (half, LANES), 1)
    for b in range(bands):
        at = (b // per) * LANES
        low = partial[:half, at : at + LANES]
        high = partial[half:, at : at + LANES]
        if b % per == 0:
            high = pltpu.roll(high, width, 1)
        else:
            low = pltpu.roll(low, width, 1)
        send[b, 0:half, :] = jnp.where(lane < width, low, high)


def edge_rows(size, moved, first_got, second_got, token, before, coeffs):
    return pl.pallas_call(
        functools.partial(edge_kernel, size),
        out_shape=jax.ShapeDtypeStruct(
            (lax.axis_size("band"), size.frames // 2 + 8, LANES), jnp.float32
        ),
        in_specs=[VMEM, VMEM, VMEM, pl.BlockSpec(memory_space=pl.ANY), VMEM, VMEM],
        out_specs=VMEM,
        scratch_shapes=[
            pltpu.VMEM((2 * size.reach, size.width), jnp.float32),
            pltpu.VMEM((3 * SEGS, size.frames), jnp.float32),
        ],
        compiler_params=pltpu.CompilerParams(vmem_limit_bytes=12 * MIB),
        cost_estimate=pl.CostEstimate(flops=4 * 10**9, bytes_accessed=10**6, transcendentals=0),
        name="edge",
    )(moved, first_got, second_got, token, before, coeffs)


def first_join_kernel(size, own, other, token, out):
    out[...] = jnp.zeros(out.shape, jnp.float32)
    out[0:1, :] = packed_sums(size, own) + packed_sums(size, other)


def join_kernel(size, *refs):
    total = refs[0][...]
    for part in refs[1:-2]:
        total = total + part[...]
    refs[-1][...] = total


def join(size, kernel, parts, token):
    return pl.pallas_call(
        functools.partial(kernel, size),
        out_shape=jax.ShapeDtypeStruct((8, LANES), jnp.float32),
        in_specs=[VMEM] * len(parts) + [pl.BlockSpec(memory_space=pl.ANY)],
        out_specs=VMEM,
        compiler_params=pltpu.CompilerParams(vmem_limit_bytes=2 * MIB),
        name="join",
    )(*parts, token)


def put_kernel(send, own, other, out):
    bands, height, _ = out.shape
    for b in range(bands):
        out[b, height - 8 : height, :] = own[...] + other[...]


def put_total(send, own, other):
    return pl.pallas_call(
        put_kernel,
        out_shape=jax.ShapeDtypeStruct(send.shape, jnp.float32),
        in_specs=[VMEM] * 3,
        out_specs=VMEM,
        input_output_aliases={0: 0},
        compiler_params=pltpu.CompilerParams(vmem_limit_bytes=2 * MIB),
        name="put",
    )(send, own, other)


def finish_kernel(frame_total, blocks, out):
    bands, height, _ = blocks.shape
    half = height - 8
    summed = blocks[0]
    for b in range(1, bands):
        summed = summed + blocks[b]
    mean_total = jnp.sum(summed[half:, :]) / frame_total
    scaled = summed[:half] / mean_total
    width = out.shape[1]
    out[0:half, :] = scaled[:, :width]
    out[half:, :] = scaled[:, width:]


def finish(blocks, frame_count):
    half = frame_count // 2
    return pl.pallas_call(
        functools.partial(finish_kernel, float(frame_count * lax.axis_size("scan"))),
        out_shape=jax.ShapeDtypeStruct((2 * half, LANES // 2), jnp.float32),
        in_specs=[VMEM],
        out_specs=VMEM,
        compiler_params=pltpu.CompilerParams(vmem_limit_bytes=8 * MIB),
        name="finish",
    )(blocks)


def upper_pair(b):
    return b ^ 1


def lower_pair(b):
    return b if b in (0, lax.axis_size("band") - 1) else ((b + 1) ^ 1) - 1


def partner_steps():
    scans, bands = lax.axis_size("scan"), lax.axis_size("band")
    around = {0: 3, 1: 2, 2: 1, 3: 0}

    def x_around(s):
        return (s // 8) * 8 + around[s // 2 % 4] * 2 + s % 2

    def z_around(s):
        return around[s // 8] * 8 + s % 8

    def same(b):
        return b

    moves = [
        [(lambda s: s ^ 1, lower_pair)],
        [(x_around, same), (lambda s: s ^ 2, same), (lambda s: s ^ 4, same)],
        [(lambda s: s ^ 8, same)],
        [(z_around, same)],
    ]
    return [
        [
            [(s * bands + b, move(s) * bands + turn(b)) for s in range(scans) for b in range(bands)]
            for move, turn in step
        ]
        for step in moves
    ]


def body(frame_codes, row_scales, row_shift, col_shift, segment_labels, mask_coeffs):
    frame_count, band_height, det_cols = frame_codes.shape
    size = Sizes(frame_count, band_height, det_cols)
    cleared, spread, wide = prepare(size, diagonals(size), row_scales, segment_labels)
    moved, total, labels_only = shift_frames(
        size, row_shift, col_shift, spread, frame_codes, wide, cleared
    )
    coeffs = mask_coeffs.reshape(3 * SEGS, MASKS)
    pairs = [(b, upper_pair(b)) for b in range(lax.axis_size("band"))]
    second_got = lax.ppermute(labels_only, "band", pairs)
    steps = partner_steps()
    cuts = [0, band_height // 4, band_height * 5 // 8, band_height]
    moments, got = None, []
    for i, step in enumerate(steps):
        got.append([lax.ppermute(total, ("scan", "band"), pairs) for pairs in step])
        if i < len(steps) - 1:
            moments = core_rows(size, moved, wide, total, moments, cuts[i], cuts[i + 1])
            kernel = first_join_kernel if i == 0 else join_kernel
            total = join(size, kernel, [total] + got[i], moments)
    send = edge_rows(size, moved, got[0][0], second_got, total, moments, coeffs)
    send = put_total(send, total, got[-1][0])
    blocks = lax.all_to_all(send, "band", 0, 0)
    return finish(blocks, frame_count)


def solution(mesh):
    return jax.shard_map(
        body,
        mesh=mesh,
        in_specs=(
            P("scan", "band", None),
            P("scan", "band"),
            P("scan"),
            P("scan"),
            P("band", None),
            P(),
        ),
        out_specs=P("scan", "band"),
        check_vma=False,
    )
```

```python
import functools

import jax
import jax.numpy as jnp
from jax import lax
from jax.experimental import pallas as pl
from jax.experimental.pallas import tpu as pltpu
from jax.sharding import PartitionSpec as P

MASKS = 512
SEGS = 128
LANES = 128
MIB = 2**20
VMEM = pl.BlockSpec(memory_space=pltpu.VMEM)
SMEM = pl.BlockSpec(memory_space=pltpu.SMEM)


class Sizes:
    def __init__(self, frame_count, band_height, det_cols):
        self.frames = frame_count
        self.rows = band_height
        self.cols = det_cols
        self.reach = band_height // 8
        self.ext = band_height + 2 * self.reach
        self.tiles = -(-det_cols // LANES)
        self.width = self.tiles * LANES
        self.pitch = frame_count + 1
        self.tall = -(-band_height // 16) * 16
        self.packed = -(-(self.reach + 3) // 16) * 16


def widened(size, labels):
    fill = jnp.full((labels.shape[0], size.width - size.cols), -1.0, jnp.float32)
    return jnp.concatenate([labels.astype(jnp.float32), fill], axis=1)


def pack(size, out, lines, labels, sums):
    high = sums.astype(jnp.bfloat16).astype(jnp.float32)
    middle = (sums - high).astype(jnp.bfloat16).astype(jnp.float32)
    lines[...] = jnp.zeros(lines.shape, jnp.float32)
    lines[0 : size.reach, :] = labels
    for k, part in enumerate([high, middle, sums - high - middle]):
        lines[size.reach + k : size.reach + k + 1, 0:LANES] = part
    out[...] = lines[...].astype(jnp.bfloat16)


def packed_sums(size, message):
    parts = message[...].astype(jnp.float32)[size.reach : size.reach + 3, 0:LANES]
    return parts[0:1] + parts[1:2] + parts[2:3]


def diagonal_kernel(size, out):
    place = lax.broadcasted_iota(jnp.int32, out.shape, 1)
    row = lax.broadcasted_iota(jnp.int32, out.shape, 0)
    chosen = (place == row) | (place == row + size.rows) | (place == row + 2 * size.rows)
    out[...] = jnp.where(chosen & (row < size.rows), 1.0, 0.0).astype(jnp.bfloat16)


def diagonals(size):
    return pl.pallas_call(
        functools.partial(diagonal_kernel, size),
        out_shape=jax.ShapeDtypeStruct((size.tall, 2 * LANES), jnp.bfloat16),
        out_specs=VMEM,
        compiler_params=pltpu.CompilerParams(vmem_limit_bytes=2 * MIB),
        cost_estimate=pl.CostEstimate(flops=10**10, bytes_accessed=10**6, transcendentals=0),
        name="diagonals",
    )()


def prepare_kernel(
    size, diagonal, scales, labels, moved, spread, wide, labels_only, split, lines
):
    frames, rows = size.frames, size.rows
    empty = jnp.zeros((frames, LANES), jnp.float32)

    def clear(e, carry):
        for t in range(size.tiles):
            moved[t, pl.ds(e * size.pitch, frames), :] = empty
            moved[t, pl.ds((e + rows) * size.pitch, frames), :] = empty
        return carry

    lax.fori_loop(0, 2 * size.reach, clear, 0, unroll=3)

    whole = scales[...]
    high = whole.astype(jnp.bfloat16).astype(jnp.float32)
    middle = (whole - high).astype(jnp.bfloat16).astype(jnp.float32)
    rest = jnp.zeros((frames, 2 * LANES - rows), jnp.float32)
    parts = [
        pltpu.roll(jnp.concatenate([part, rest], axis=1), k * rows, 1)
        for k, part in enumerate([high, middle, whole - high - middle])
    ]
    split[...] = parts[0] + parts[1] + parts[2]
    tall = size.tall
    group = 8
    ones = jnp.ones((2 * LANES, LANES), jnp.bfloat16)

    def spread_group(i, carry):
        chosen = []
        for j in range(group):
            line = split[pl.ds(i * group + j, 1), :]
            line = jnp.broadcast_to(line, (16, 2 * LANES)).astype(jnp.bfloat16)
            chosen.append(jnp.concatenate([line] * (tall // 16), axis=0) * diagonal[...])
        at = pl.multiple_of(i * (group * tall), 8)
        spread[pl.ds(at, group * tall), :] = jnp.dot(
            jnp.concatenate(chosen, axis=0), ones, preferred_element_type=jnp.float32
        )
        return carry

    lax.fori_loop(0, frames // group, spread_group, 0, unroll=8)
    wide[...] = widened(size, labels[...])
    top, bottom = wide[0 : size.reach, :], wide[rows - size.reach : rows, :]
    wanted = jnp.where(lax.axis_index("band") % 2 == 1, top, bottom)
    pack(size, labels_only, lines, wanted, jnp.zeros((1, LANES), jnp.float32))


def prepare(size, diagonal, scales, labels):
    return pl.pallas_call(
        functools.partial(prepare_kernel, size),
        out_shape=[
            jax.ShapeDtypeStruct((size.tiles, size.ext * size.pitch, LANES), jnp.float32),
            jax.ShapeDtypeStruct((size.frames * size.tall, LANES), jnp.float32),
            jax.ShapeDtypeStruct((size.rows, size.width), jnp.float32),
            jax.ShapeDtypeStruct((size.packed, size.width), jnp.bfloat16),
        ],
        in_specs=[VMEM] * 3,
        out_specs=[VMEM] * 4,
        scratch_shapes=[
            pltpu.VMEM((size.frames, 2 * LANES), jnp.float32),
            pltpu.VMEM((size.packed, size.width), jnp.float32),
        ],
        compiler_params=pltpu.CompilerParams(vmem_limit_bytes=8 * MIB),
        cost_estimate=pl.CostEstimate(flops=5 * 10**8, bytes_accessed=10**6, transcendentals=0),
        name="prepare",
    )(diagonal, scales, labels)


def shift_kernel(
    size, row_shift, col_shift, spread, codes, wide, cleared, moved, payload, total, lines
):
    frames, rows, cols, tiles, reach = size.frames, size.rows, size.cols, size.tiles, size.reach
    total[...] = jnp.zeros((rows, LANES), jnp.float32)
    whole_lane = lax.broadcasted_iota(jnp.int32, (rows, LANES), 1)
    lane = whole_lane.astype(jnp.float32).astype(jnp.bfloat16)
    source = lax.broadcasted_iota(jnp.int32, (rows, LANES), 0)
    band = lax.axis_index("band")
    zero = jnp.zeros((rows, LANES), jnp.bfloat16)

    def shift_frame(f, carry):
        down, right = row_shift[f], col_shift[f]
        turn = jnp.where(right < 0, right + LANES, right)
        left_end = jnp.where(right < 0, 0, turn).astype(jnp.float32).astype(jnp.bfloat16)
        right_start = jnp.where(right < 0, turn, LANES).astype(jnp.float32).astype(jnp.bfloat16)
        from_left = lane < left_end
        from_right = lane >= right_start
        scale_f = spread[pl.ds(pl.multiple_of(f * size.tall, 8), rows), :]
        turned = [zero]
        for t in range(tiles):
            upper = min(cols, (t + 1) * LANES)
            value = codes[f, :, t * LANES : upper].astype(jnp.float32)
            if upper < (t + 1) * LANES:
                fill = jnp.zeros((rows, (t + 1) * LANES - upper), jnp.float32)
                value = jnp.concatenate([value, fill], axis=1)
            turned.append(pltpu.roll((value * scale_f).astype(jnp.bfloat16), turn, 1))
        turned.append(zero)
        start = (reach + down) * size.pitch + f
        row_sum = jnp.zeros((rows, LANES), jnp.float32)
        for t in range(tiles):
            out = jnp.where(
                from_left, turned[t], jnp.where(from_right, turned[t + 2], turned[t + 1])
            ).astype(jnp.float32)
            moved[t, pl.ds(start, rows, stride=size.pitch), :] = out
            if (t + 1) * LANES > cols:
                out = jnp.where(whole_lane < cols - t * LANES, out, 0.0)
            row_sum = row_sum + out
        target = source + (band * rows + down)
        total[...] += jnp.where((target >= 0) & (target < cols), row_sum, 0.0)
        return carry

    lax.fori_loop(0, frames, shift_frame, 0, unroll=8)
    top, bottom = wide[0:reach, :], wide[rows - reach : rows, :]
    sums = jnp.sum(total[...], axis=0, keepdims=True)
    pack(size, payload, lines, jnp.where(band % 2 == 1, bottom, top), sums)


def shift_frames(size, row_shift, col_shift, spread, codes, wide, cleared):
    return pl.pallas_call(
        functools.partial(shift_kernel, size),
        out_shape=[
            jax.ShapeDtypeStruct(cleared.shape, jnp.float32),
            jax.ShapeDtypeStruct((size.packed, size.width), jnp.bfloat16),
        ],
        in_specs=[SMEM] * 2 + [VMEM] * 4,
        out_specs=[VMEM] * 2,
        scratch_shapes=[
            pltpu.VMEM((size.rows, LANES), jnp.float32),
            pltpu.VMEM((size.packed, size.width), jnp.float32),
        ],
        input_output_aliases={5: 0},
        compiler_params=pltpu.CompilerParams(vmem_limit_bytes=12 * MIB),
        cost_estimate=pl.CostEstimate(flops=6 * 10**9, bytes_accessed=10**6, transcendentals=0),
        name="shift",
    )(row_shift, col_shift, spread, codes, wide, cleared)


def table_consts(size):
    segment = lax.broadcasted_iota(jnp.int32, (16, size.width), 0)
    column = lax.broadcasted_iota(jnp.int32, (16, size.width), 1).astype(jnp.float32)
    xcoord = ((column + 0.5) / size.cols - 0.5).astype(jnp.bfloat16)
    ids = [
        (segment + 16 * k).astype(jnp.float32).astype(jnp.bfloat16) for k in range(SEGS // 16)
    ]
    return ids, xcoord


def add_row(size, consts, label_row, values, moments, e):
    ids, xcoord = consts
    zero = jnp.zeros((16, size.width), jnp.bfloat16)
    one = jnp.ones((16, size.width), jnp.bfloat16)
    label = jnp.broadcast_to(label_row, (16, size.width)).astype(jnp.bfloat16)
    plain, by_x = [], []
    for k in range(SEGS // 16):
        same = label == ids[k]
        plain.append(jnp.where(same, one, zero))
        by_x.append(jnp.where(same, xcoord, zero))
    table = jnp.concatenate(plain + by_x, axis=0)
    sums = lax.dot_general(
        table, values, (((1,), (1,)), ((), ())), preferred_element_type=jnp.float32
    )
    first_row = lax.axis_index("band") * size.rows
    offset = (first_row + e - size.reach).astype(jnp.float32)
    ycoord = ((offset + 0.5) / size.cols - 0.5).astype(jnp.bfloat16).astype(jnp.float32)
    moments[0:SEGS, :] += sums[0:SEGS]
    moments[SEGS : 2 * SEGS, :] += sums[0:SEGS] * ycoord
    moments[2 * SEGS : 3 * SEGS, :] += sums[SEGS : 2 * SEGS]


def values_of(size, moved, e):
    base = e * size.pitch
    tiles = [
        moved[t, pl.ds(base, size.frames), :].astype(jnp.bfloat16) for t in range(size.tiles)
    ]
    return jnp.concatenate(tiles, axis=1)


def core_kernel(size, first, last, started, moved, wide, token, *refs):
    if started:
        before, moments = refs
        moments[...] = before[...]
    else:
        (moments,) = refs
        moments[...] = jnp.zeros(moments.shape, jnp.float32)
    consts = table_consts(size)

    def step(r, carry):
        e = r + size.reach
        add_row(size, consts, wide[pl.ds(r, 1), :], values_of(size, moved, e), moments, e)
        return carry

    lax.fori_loop(first, last, step, 0, unroll=9)


def core_rows(size, moved, wide, token, before, first, last):
    args = [moved, wide, token] + ([] if before is None else [before])
    specs = [VMEM, VMEM, pl.BlockSpec(memory_space=pl.ANY)] + [VMEM] * (len(args) - 3)
    return pl.pallas_call(
        functools.partial(core_kernel, size, first, last, before is not None),
        out_shape=jax.ShapeDtypeStruct((3 * SEGS, size.frames), jnp.float32),
        in_specs=specs,
        out_specs=VMEM,
        compiler_params=pltpu.CompilerParams(vmem_limit_bytes=8 * MIB),
        cost_estimate=pl.CostEstimate(flops=4 * 10**9, bytes_accessed=10**6, transcendentals=0),
        name="core",
    )(*args)


def edge_kernel(size, moved, first_got, second_got, token, before, coeffs, send, wide, moments):
    frames, rows, reach = size.frames, size.rows, size.reach
    moments[...] = before[...]
    band, bands = lax.axis_index("band"), lax.axis_size("band")
    odd = band % 2 == 1
    first = first_got[...].astype(jnp.float32)[0:reach, :]
    second = second_got[...].astype(jnp.float32)[0:reach, :]
    wide[0:reach, :] = jnp.where(odd, second, first)
    wide[reach : 2 * reach, :] = jnp.where(odd, first, second)
    nothing = jnp.full((reach, size.width), -1.0, jnp.float32)

    @pl.when(band == 0)
    def _():
        wide[0:reach, :] = nothing

    @pl.when(band == bands - 1)
    def _():
        wide[reach : 2 * reach, :] = nothing

    consts = table_consts(size)

    def step(r, carry):
        e = jnp.where(r < reach, r, r + rows)
        add_row(size, consts, wide[pl.ds(r, 1), :], values_of(size, moved, e), moments, e)
        return carry

    lax.fori_loop(0, 2 * reach, step, 0, unroll=9)
    partial = jnp.dot(
        moments[...].T,
        coeffs[...],
        precision=lax.Precision.HIGHEST,
        preferred_element_type=jnp.float32,
    )
    half = frames // 2
    width = MASKS // bands
    per = LANES // width
    lane = lax.broadcasted_iota(jnp.int32, (half, LANES), 1)
    for b in range(bands):
        at = (b // per) * LANES
        low = partial[:half, at : at + LANES]
        high = partial[half:, at : at + LANES]
        if b % per == 0:
            high = pltpu.roll(high, width, 1)
        else:
            low = pltpu.roll(low, width, 1)
        send[b, 0:half, :] = jnp.where(lane < width, low, high)


def edge_rows(size, moved, first_got, second_got, token, before, coeffs):
    return pl.pallas_call(
        functools.partial(edge_kernel, size),
        out_shape=jax.ShapeDtypeStruct(
            (lax.axis_size("band"), size.frames // 2 + 8, LANES), jnp.float32
        ),
        in_specs=[VMEM, VMEM, VMEM, pl.BlockSpec(memory_space=pl.ANY), VMEM, VMEM],
        out_specs=VMEM,
        scratch_shapes=[
            pltpu.VMEM((2 * size.reach, size.width), jnp.float32),
            pltpu.VMEM((3 * SEGS, size.frames), jnp.float32),
        ],
        compiler_params=pltpu.CompilerParams(vmem_limit_bytes=12 * MIB),
        cost_estimate=pl.CostEstimate(flops=4 * 10**9, bytes_accessed=10**6, transcendentals=0),
        name="edge",
    )(moved, first_got, second_got, token, before, coeffs)


def first_join_kernel(size, own, other, token, out):
    out[...] = jnp.zeros(out.shape, jnp.float32)
    out[0:1, :] = packed_sums(size, own) + packed_sums(size, other)


def join_kernel(size, *refs):
    total = refs[0][...]
    for part in refs[1:-2]:
        total = total + part[...]
    refs[-1][...] = total


def join(size, kernel, parts, token):
    return pl.pallas_call(
        functools.partial(kernel, size),
        out_shape=jax.ShapeDtypeStruct((8, LANES), jnp.float32),
        in_specs=[VMEM] * len(parts) + [pl.BlockSpec(memory_space=pl.ANY)],
        out_specs=VMEM,
        compiler_params=pltpu.CompilerParams(vmem_limit_bytes=2 * MIB),
        name="join",
    )(*parts, token)


def put_kernel(send, own, other, out):
    bands, height, _ = out.shape
    for b in range(bands):
        out[b, height - 8 : height, :] = own[...] + other[...]


def put_total(send, own, other):
    return pl.pallas_call(
        put_kernel,
        out_shape=jax.ShapeDtypeStruct(send.shape, jnp.float32),
        in_specs=[VMEM] * 3,
        out_specs=VMEM,
        input_output_aliases={0: 0},
        compiler_params=pltpu.CompilerParams(vmem_limit_bytes=2 * MIB),
        name="put",
    )(send, own, other)


def finish_kernel(frame_total, blocks, out):
    bands, height, _ = blocks.shape
    half = height - 8
    summed = blocks[0]
    for b in range(1, bands):
        summed = summed + blocks[b]
    mean_total = jnp.sum(summed[half:, :]) / frame_total
    scaled = summed[:half] / mean_total
    width = out.shape[1]
    out[0:half, :] = scaled[:, :width]
    out[half:, :] = scaled[:, width:]


def finish(blocks, frame_count):
    half = frame_count // 2
    return pl.pallas_call(
        functools.partial(finish_kernel, float(frame_count * lax.axis_size("scan"))),
        out_shape=jax.ShapeDtypeStruct((2 * half, LANES // 2), jnp.float32),
        in_specs=[VMEM],
        out_specs=VMEM,
        compiler_params=pltpu.CompilerParams(vmem_limit_bytes=8 * MIB),
        name="finish",
    )(blocks)


def upper_pair(b):
    return b ^ 1


def lower_pair(b):
    return b if b in (0, lax.axis_size("band") - 1) else ((b + 1) ^ 1) - 1


def partner_steps():
    scans, bands = lax.axis_size("scan"), lax.axis_size("band")
    around = {0: 3, 1: 2, 2: 1, 3: 0}

    def x_around(s):
        return (s // 8) * 8 + around[s // 2 % 4] * 2 + s % 2

    def z_around(s):
        return around[s // 8] * 8 + s % 8

    def same(b):
        return b

    moves = [
        [(lambda s: s ^ 1, lower_pair)],
        [(x_around, same), (lambda s: s ^ 2, same), (lambda s: s ^ 4, same)],
        [(lambda s: s ^ 8, same)],
        [(z_around, same)],
    ]
    return [
        [
            [(s * bands + b, move(s) * bands + turn(b)) for s in range(scans) for b in range(bands)]
            for move, turn in step
        ]
        for step in moves
    ]


def body(frame_codes, row_scales, row_shift, col_shift, segment_labels, mask_coeffs):
    frame_count, band_height, det_cols = frame_codes.shape
    size = Sizes(frame_count, band_height, det_cols)
    cleared, spread, wide, labels_only = prepare(
        size, diagonals(size), row_scales, segment_labels
    )
    moved, total = shift_frames(size, row_shift, col_shift, spread, frame_codes, wide, cleared)
    coeffs = mask_coeffs.reshape(3 * SEGS, MASKS)
    pairs = [(b, upper_pair(b)) for b in range(lax.axis_size("band"))]
    second_got = lax.ppermute(labels_only, "band", pairs)
    steps = partner_steps()
    cuts = [0, band_height // 4, band_height * 5 // 8, band_height]
    moments, got = None, []
    for i, step in enumerate(steps):
        got.append([lax.ppermute(total, ("scan", "band"), pairs) for pairs in step])
        if i < len(steps) - 1:
            moments = core_rows(size, moved, wide, total, moments, cuts[i], cuts[i + 1])
            kernel = first_join_kernel if i == 0 else join_kernel
            total = join(size, kernel, [total] + got[i], moments)
    send = edge_rows(size, moved, got[0][0], second_got, total, moments, coeffs)
    send = put_total(send, total, got[-1][0])
    blocks = lax.all_to_all(send, "band", 0, 0)
    return finish(blocks, frame_count)


def solution(mesh):
    return jax.shard_map(
        body,
        mesh=mesh,
        in_specs=(
            P("scan", "band", None),
            P("scan", "band"),
            P("scan"),
            P("scan"),
            P("band", None),
            P(),
        ),
        out_specs=P("scan", "band"),
        check_vma=False,
    )
```

```python
import functools

import jax
import jax.numpy as jnp
from jax import lax
from jax.experimental import pallas as pl
from jax.experimental.pallas import tpu as pltpu
from jax.sharding import PartitionSpec as P

MASKS = 512
SEGS = 128
LANES = 128
MIB = 2**20
VMEM = pl.BlockSpec(memory_space=pltpu.VMEM)
SMEM = pl.BlockSpec(memory_space=pltpu.SMEM)


class Sizes:
    def __init__(self, frame_count, band_height, det_cols):
        self.frames = frame_count
        self.rows = band_height
        self.cols = det_cols
        self.reach = band_height // 8
        self.ext = band_height + 2 * self.reach
        self.tiles = -(-det_cols // LANES)
        self.width = self.tiles * LANES
        self.pitch = frame_count + 1
        self.lines = -(-(self.ext + 1) * self.pitch // 8) * 8
        self.tall = -(-band_height // 16) * 16
        self.packed = -(-(self.reach + 3) // 16) * 16


def widened(size, labels):
    fill = jnp.full((labels.shape[0], size.width - size.cols), -1.0, jnp.float32)
    return jnp.concatenate([labels.astype(jnp.float32), fill], axis=1)


def pack(size, out, lines, labels, sums):
    high = sums.astype(jnp.bfloat16).astype(jnp.float32)
    middle = (sums - high).astype(jnp.bfloat16).astype(jnp.float32)
    lines[...] = jnp.zeros(lines.shape, jnp.float32)
    lines[0 : size.reach, :] = labels
    for k, part in enumerate([high, middle, sums - high - middle]):
        lines[size.reach + k : size.reach + k + 1, 0:LANES] = part
    out[...] = lines[...].astype(jnp.bfloat16)


def packed_sums(size, message):
    parts = message[...].astype(jnp.float32)[size.reach : size.reach + 3, 0:LANES]
    return parts[0:1] + parts[1:2] + parts[2:3]


def diagonal_kernel(size, out):
    place = lax.broadcasted_iota(jnp.int32, out.shape, 1)
    row = lax.broadcasted_iota(jnp.int32, out.shape, 0)
    chosen = (place == row) | (place == row + size.rows) | (place == row + 2 * size.rows)
    out[...] = jnp.where(chosen & (row < size.rows), 1.0, 0.0).astype(jnp.bfloat16)


def diagonals(size):
    return pl.pallas_call(
        functools.partial(diagonal_kernel, size),
        out_shape=jax.ShapeDtypeStruct((size.tall, 2 * LANES), jnp.bfloat16),
        out_specs=VMEM,
        compiler_params=pltpu.CompilerParams(vmem_limit_bytes=2 * MIB),
        cost_estimate=pl.CostEstimate(flops=10**10, bytes_accessed=10**6, transcendentals=0),
        name="diagonals",
    )()


def prepare_kernel(
    size, diagonal, scales, labels, moved, spread, wide, labels_only, split, lines
):
    frames, rows = size.frames, size.rows
    empty = jnp.zeros((frames, LANES), jnp.float32)

    def clear(e, carry):
        for t in range(size.tiles):
            moved[t, pl.ds(e * size.pitch, frames), :] = empty
            moved[t, pl.ds((e + rows) * size.pitch, frames), :] = empty
        return carry

    lax.fori_loop(0, 2 * size.reach, clear, 0, unroll=3)

    whole = scales[...]
    high = whole.astype(jnp.bfloat16).astype(jnp.float32)
    middle = (whole - high).astype(jnp.bfloat16).astype(jnp.float32)
    rest = jnp.zeros((frames, 2 * LANES - rows), jnp.float32)
    parts = [
        pltpu.roll(jnp.concatenate([part, rest], axis=1), k * rows, 1)
        for k, part in enumerate([high, middle, whole - high - middle])
    ]
    split[...] = parts[0] + parts[1] + parts[2]
    tall = size.tall
    group = 8
    ones = jnp.ones((2 * LANES, LANES), jnp.bfloat16)

    def spread_group(i, carry):
        chosen = []
        for j in range(group):
            line = split[pl.ds(i * group + j, 1), :]
            line = jnp.broadcast_to(line, (16, 2 * LANES)).astype(jnp.bfloat16)
            chosen.append(jnp.concatenate([line] * (tall // 16), axis=0) * diagonal[...])
        at = pl.multiple_of(i * (group * tall), 8)
        spread[pl.ds(at, group * tall), :] = jnp.dot(
            jnp.concatenate(chosen, axis=0), ones, preferred_element_type=jnp.float32
        )
        return carry

    lax.fori_loop(0, frames // group, spread_group, 0, unroll=8)
    wide[...] = widened(size, labels[...])
    top, bottom = wide[0 : size.reach, :], wide[rows - size.reach : rows, :]
    wanted = jnp.where(lax.axis_index("band") % 2 == 1, top, bottom)
    pack(size, labels_only, lines, wanted, jnp.zeros((1, LANES), jnp.float32))


def prepare(size, diagonal, scales, labels):
    return pl.pallas_call(
        functools.partial(prepare_kernel, size),
        out_shape=[
            jax.ShapeDtypeStruct((size.tiles, size.lines, LANES), jnp.float32),
            jax.ShapeDtypeStruct((size.frames * size.tall, LANES), jnp.float32),
            jax.ShapeDtypeStruct((size.rows, size.width), jnp.float32),
            jax.ShapeDtypeStruct((size.packed, size.width), jnp.bfloat16),
        ],
        in_specs=[VMEM] * 3,
        out_specs=[VMEM] * 4,
        scratch_shapes=[
            pltpu.VMEM((size.frames, 2 * LANES), jnp.float32),
            pltpu.VMEM((size.packed, size.width), jnp.float32),
        ],
        compiler_params=pltpu.CompilerParams(vmem_limit_bytes=8 * MIB),
        cost_estimate=pl.CostEstimate(flops=5 * 10**8, bytes_accessed=10**6, transcendentals=0),
        name="prepare",
    )(diagonal, scales, labels)


def shift_kernel(
    size, row_shift, col_shift, spread, codes, wide, cleared, moved, payload, total, lines
):
    frames, rows, cols, tiles, reach = size.frames, size.rows, size.cols, size.tiles, size.reach
    total[...] = jnp.zeros((rows, LANES), jnp.float32)
    whole_lane = lax.broadcasted_iota(jnp.int32, (rows, LANES), 1)
    lane = whole_lane.astype(jnp.float32).astype(jnp.bfloat16)
    source = lax.broadcasted_iota(jnp.int32, (rows, LANES), 0)
    band = lax.axis_index("band")
    zero = jnp.zeros((rows, LANES), jnp.bfloat16)

    def shift_frame(f, carry):
        down, right = row_shift[f], col_shift[f]
        turn = jnp.where(right < 0, right + LANES, right)
        left_end = jnp.where(right < 0, 0, turn).astype(jnp.float32).astype(jnp.bfloat16)
        right_start = jnp.where(right < 0, turn, LANES).astype(jnp.float32).astype(jnp.bfloat16)
        from_left = lane < left_end
        from_right = lane >= right_start
        scale_f = spread[pl.ds(pl.multiple_of(f * size.tall, 8), rows), :]
        turned = [zero]
        for t in range(tiles):
            upper = min(cols, (t + 1) * LANES)
            value = codes[f, :, t * LANES : upper].astype(jnp.float32)
            if upper < (t + 1) * LANES:
                fill = jnp.zeros((rows, (t + 1) * LANES - upper), jnp.float32)
                value = jnp.concatenate([value, fill], axis=1)
            turned.append(pltpu.roll((value * scale_f).astype(jnp.bfloat16), turn, 1))
        turned.append(zero)
        start = (reach + down) * size.pitch + f
        row_sum = jnp.zeros((rows, LANES), jnp.float32)
        for t in range(tiles):
            out = jnp.where(
                from_left, turned[t], jnp.where(from_right, turned[t + 2], turned[t + 1])
            ).astype(jnp.float32)
            moved[t, pl.ds(start, rows, stride=size.pitch), :] = out
            if (t + 1) * LANES > cols:
                out = jnp.where(whole_lane < cols - t * LANES, out, 0.0)
            row_sum = row_sum + out
        target = source + (band * rows + down)
        total[...] += jnp.where((target >= 0) & (target < cols), row_sum, 0.0)
        return carry

    lax.fori_loop(0, frames, shift_frame, 0, unroll=8)
    top, bottom = wide[0:reach, :], wide[rows - reach : rows, :]
    sums = jnp.sum(total[...], axis=0, keepdims=True)
    pack(size, payload, lines, jnp.where(band % 2 == 1, bottom, top), sums)


def shift_frames(size, row_shift, col_shift, spread, codes, wide, cleared):
    return pl.pallas_call(
        functools.partial(shift_kernel, size),
        out_shape=[
            jax.ShapeDtypeStruct(cleared.shape, jnp.float32),
            jax.ShapeDtypeStruct((size.packed, size.width), jnp.bfloat16),
        ],
        in_specs=[SMEM] * 2 + [VMEM] * 4,
        out_specs=[VMEM] * 2,
        scratch_shapes=[
            pltpu.VMEM((size.rows, LANES), jnp.float32),
            pltpu.VMEM((size.packed, size.width), jnp.float32),
        ],
        input_output_aliases={5: 0},
        compiler_params=pltpu.CompilerParams(vmem_limit_bytes=12 * MIB),
        cost_estimate=pl.CostEstimate(flops=6 * 10**9, bytes_accessed=10**6, transcendentals=0),
        name="shift",
    )(row_shift, col_shift, spread, codes, wide, cleared)


def table_consts(size):
    segment = lax.broadcasted_iota(jnp.int32, (16, size.width), 0)
    column = lax.broadcasted_iota(jnp.int32, (16, size.width), 1).astype(jnp.float32)
    xcoord = ((column + 0.5) / size.cols - 0.5).astype(jnp.bfloat16)
    ids = [
        (segment + 16 * k).astype(jnp.float32).astype(jnp.bfloat16) for k in range(SEGS // 16)
    ]
    return ids, xcoord


def add_row(size, consts, label_row, values, moments, e):
    ids, xcoord = consts
    zero = jnp.zeros((16, size.width), jnp.bfloat16)
    one = jnp.ones((16, size.width), jnp.bfloat16)
    label = jnp.broadcast_to(label_row, (16, size.width)).astype(jnp.bfloat16)
    plain, by_x = [], []
    for k in range(SEGS // 16):
        same = label == ids[k]
        plain.append(jnp.where(same, one, zero))
        by_x.append(jnp.where(same, xcoord, zero))
    table = jnp.concatenate(plain + by_x, axis=0)
    sums = lax.dot_general(
        table, values, (((1,), (1,)), ((), ())), preferred_element_type=jnp.float32
    )
    first_row = lax.axis_index("band") * size.rows
    offset = (first_row + e - size.reach).astype(jnp.float32)
    ycoord = ((offset + 0.5) / size.cols - 0.5).astype(jnp.bfloat16).astype(jnp.float32)
    moments[0:SEGS, :] += sums[0:SEGS]
    moments[SEGS : 2 * SEGS, :] += sums[0:SEGS] * ycoord
    moments[2 * SEGS : 3 * SEGS, :] += sums[SEGS : 2 * SEGS]


def values_of(size, moved, e):
    base = e * size.pitch
    tiles = [
        moved[t, pl.ds(base, size.frames), :].astype(jnp.bfloat16) for t in range(size.tiles)
    ]
    return jnp.concatenate(tiles, axis=1)


def core_kernel(size, first, last, started, moved, wide, token, *refs):
    if started:
        before, moments = refs
        moments[...] = before[...]
    else:
        (moments,) = refs
        moments[...] = jnp.zeros(moments.shape, jnp.float32)
    consts = table_consts(size)

    def step(r, carry):
        e = r + size.reach
        add_row(size, consts, wide[pl.ds(r, 1), :], values_of(size, moved, e), moments, e)
        return carry

    lax.fori_loop(first, last, step, 0, unroll=9)


def core_rows(size, moved, wide, token, before, first, last):
    args = [moved, wide, token] + ([] if before is None else [before])
    specs = [VMEM, VMEM, pl.BlockSpec(memory_space=pl.ANY)] + [VMEM] * (len(args) - 3)
    return pl.pallas_call(
        functools.partial(core_kernel, size, first, last, before is not None),
        out_shape=jax.ShapeDtypeStruct((3 * SEGS, size.frames), jnp.float32),
        in_specs=specs,
        out_specs=VMEM,
        compiler_params=pltpu.CompilerParams(vmem_limit_bytes=8 * MIB),
        cost_estimate=pl.CostEstimate(flops=4 * 10**9, bytes_accessed=10**6, transcendentals=0),
        name="core",
    )(*args)


def edge_kernel(size, moved, first_got, second_got, token, before, coeffs, send, wide, moments):
    frames, rows, reach = size.frames, size.rows, size.reach
    moments[...] = before[...]
    band, bands = lax.axis_index("band"), lax.axis_size("band")
    odd = band % 2 == 1
    first = first_got[...].astype(jnp.float32)[0:reach, :]
    second = second_got[...].astype(jnp.float32)[0:reach, :]
    wide[0:reach, :] = jnp.where(odd, second, first)
    wide[reach : 2 * reach, :] = jnp.where(odd, first, second)
    nothing = jnp.full((reach, size.width), -1.0, jnp.float32)

    @pl.when(band == 0)
    def _():
        wide[0:reach, :] = nothing

    @pl.when(band == bands - 1)
    def _():
        wide[reach : 2 * reach, :] = nothing

    consts = table_consts(size)

    def step(r, carry):
        e = jnp.where(r < reach, r, r + rows)
        add_row(size, consts, wide[pl.ds(r, 1), :], values_of(size, moved, e), moments, e)
        return carry

    lax.fori_loop(0, 2 * reach, step, 0, unroll=9)
    partial = jnp.dot(
        moments[...].T,
        coeffs[...],
        precision=lax.Precision.HIGHEST,
        preferred_element_type=jnp.float32,
    )
    half = frames // 2
    width = MASKS // bands
    per = LANES // width
    lane = lax.broadcasted_iota(jnp.int32, (half, LANES), 1)
    for b in range(bands):
        at = (b // per) * LANES
        low = partial[:half, at : at + LANES]
        high = partial[half:, at : at + LANES]
        if b % per == 0:
            high = pltpu.roll(high, width, 1)
        else:
            low = pltpu.roll(low, width, 1)
        send[b, 0:half, :] = jnp.where(lane < width, low, high)


def edge_rows(size, moved, first_got, second_got, token, before, coeffs):
    return pl.pallas_call(
        functools.partial(edge_kernel, size),
        out_shape=jax.ShapeDtypeStruct(
            (lax.axis_size("band"), size.frames // 2 + 8, LANES), jnp.float32
        ),
        in_specs=[VMEM, VMEM, VMEM, pl.BlockSpec(memory_space=pl.ANY), VMEM, VMEM],
        out_specs=VMEM,
        scratch_shapes=[
            pltpu.VMEM((2 * size.reach, size.width), jnp.float32),
            pltpu.VMEM((3 * SEGS, size.frames), jnp.float32),
        ],
        compiler_params=pltpu.CompilerParams(vmem_limit_bytes=12 * MIB),
        cost_estimate=pl.CostEstimate(flops=4 * 10**9, bytes_accessed=10**6, transcendentals=0),
        name="edge",
    )(moved, first_got, second_got, token, before, coeffs)


def first_join_kernel(size, own, other, token, out):
    out[...] = jnp.zeros(out.shape, jnp.float32)
    out[0:1, :] = packed_sums(size, own) + packed_sums(size, other)


def join_kernel(size, *refs):
    total = refs[0][...]
    for part in refs[1:-2]:
        total = total + part[...]
    refs[-1][...] = total


def join(size, kernel, parts, token):
    return pl.pallas_call(
        functools.partial(kernel, size),
        out_shape=jax.ShapeDtypeStruct((8, LANES), jnp.float32),
        in_specs=[VMEM] * len(parts) + [pl.BlockSpec(memory_space=pl.ANY)],
        out_specs=VMEM,
        compiler_params=pltpu.CompilerParams(vmem_limit_bytes=2 * MIB),
        name="join",
    )(*parts, token)


def put_kernel(send, own, other, out):
    bands, height, _ = out.shape
    for b in range(bands):
        out[b, height - 8 : height, :] = own[...] + other[...]


def put_total(send, own, other):
    return pl.pallas_call(
        put_kernel,
        out_shape=jax.ShapeDtypeStruct(send.shape, jnp.float32),
        in_specs=[VMEM] * 3,
        out_specs=VMEM,
        input_output_aliases={0: 0},
        compiler_params=pltpu.CompilerParams(vmem_limit_bytes=2 * MIB),
        name="put",
    )(send, own, other)


def finish_kernel(frame_total, blocks, out):
    bands, height, _ = blocks.shape
    half = height - 8
    summed = blocks[0]
    for b in range(1, bands):
        summed = summed + blocks[b]
    mean_total = jnp.sum(summed[half:, :]) / frame_total
    scaled = summed[:half] / mean_total
    width = out.shape[1]
    out[0:half, :] = scaled[:, :width]
    out[half:, :] = scaled[:, width:]


def finish(blocks, frame_count):
    half = frame_count // 2
    return pl.pallas_call(
        functools.partial(finish_kernel, float(frame_count * lax.axis_size("scan"))),
        out_shape=jax.ShapeDtypeStruct((2 * half, LANES // 2), jnp.float32),
        in_specs=[VMEM],
        out_specs=VMEM,
        compiler_params=pltpu.CompilerParams(vmem_limit_bytes=8 * MIB),
        name="finish",
    )(blocks)


def upper_pair(b):
    return b ^ 1


def lower_pair(b):
    return b if b in (0, lax.axis_size("band") - 1) else ((b + 1) ^ 1) - 1


def partner_steps():
    scans, bands = lax.axis_size("scan"), lax.axis_size("band")
    around = {0: 3, 1: 2, 2: 1, 3: 0}

    def x_around(s):
        return (s // 8) * 8 + around[s // 2 % 4] * 2 + s % 2

    def z_around(s):
        return around[s // 8] * 8 + s % 8

    def same(b):
        return b

    moves = [
        [(lambda s: s ^ 1, lower_pair)],
        [(x_around, same), (lambda s: s ^ 2, same), (lambda s: s ^ 4, same)],
        [(lambda s: s ^ 8, same)],
        [(z_around, same)],
    ]
    return [
        [
            [(s * bands + b, move(s) * bands + turn(b)) for s in range(scans) for b in range(bands)]
            for move, turn in step
        ]
        for step in moves
    ]


def body(frame_codes, row_scales, row_shift, col_shift, segment_labels, mask_coeffs):
    frame_count, band_height, det_cols = frame_codes.shape
    size = Sizes(frame_count, band_height, det_cols)
    cleared, spread, wide, labels_only = prepare(
        size, diagonals(size), row_scales, segment_labels
    )
    moved, total = shift_frames(size, row_shift, col_shift, spread, frame_codes, wide, cleared)
    coeffs = mask_coeffs.reshape(3 * SEGS, MASKS)
    pairs = [(b, upper_pair(b)) for b in range(lax.axis_size("band"))]
    second_got = lax.ppermute(labels_only, "band", pairs)
    steps = partner_steps()
    cuts = [0, band_height // 4, band_height * 5 // 8, band_height]
    moments, got = None, []
    for i, step in enumerate(steps):
        got.append([lax.ppermute(total, ("scan", "band"), pairs) for pairs in step])
        if i < len(steps) - 1:
            moments = core_rows(size, moved, wide, total, moments, cuts[i], cuts[i + 1])
            kernel = first_join_kernel if i == 0 else join_kernel
            total = join(size, kernel, [total] + got[i], moments)
    send = edge_rows(size, moved, got[0][0], second_got, total, moments, coeffs)
    send = put_total(send, total, got[-1][0])
    blocks = lax.all_to_all(send, "band", 0, 0)
    return finish(blocks, frame_count)


def solution(mesh):
    return jax.shard_map(
        body,
        mesh=mesh,
        in_specs=(
            P("scan", "band", None),
            P("scan", "band"),
            P("scan"),
            P("scan"),
            P("band", None),
            P(),
        ),
        out_specs=P("scan", "band"),
        check_vma=False,
    )
```

```python
import functools

import jax
import jax.numpy as jnp
from jax import lax
from jax.experimental import pallas as pl
from jax.experimental.pallas import tpu as pltpu
from jax.sharding import PartitionSpec as P

MASKS = 512
SEGS = 128
LANES = 128
MIB = 2**20
VMEM = pl.BlockSpec(memory_space=pltpu.VMEM)
SMEM = pl.BlockSpec(memory_space=pltpu.SMEM)


class Sizes:
    def __init__(self, frame_count, band_height, det_cols):
        self.frames = frame_count
        self.rows = band_height
        self.cols = det_cols
        self.reach = band_height // 8
        self.ext = band_height + 2 * self.reach
        self.tiles = -(-det_cols // LANES)
        self.width = self.tiles * LANES
        self.pitch = frame_count + 1
        self.lines = -(-(self.ext + 1) * self.pitch // 8) * 8
        self.tall = -(-band_height // 16) * 16
        self.packed = -(-(self.reach + 3) // 16) * 16


def widened(size, labels):
    fill = jnp.full((labels.shape[0], size.width - size.cols), -1.0, jnp.float32)
    return jnp.concatenate([labels.astype(jnp.float32), fill], axis=1)


def pack(size, out, lines, labels, sums):
    high = sums.astype(jnp.bfloat16).astype(jnp.float32)
    middle = (sums - high).astype(jnp.bfloat16).astype(jnp.float32)
    lines[...] = jnp.zeros(lines.shape, jnp.float32)
    lines[0 : size.reach, :] = labels
    for k, part in enumerate([high, middle, sums - high - middle]):
        lines[size.reach + k : size.reach + k + 1, 0:LANES] = part
    out[...] = lines[...].astype(jnp.bfloat16)


def packed_sums(size, message):
    parts = message[...].astype(jnp.float32)[size.reach : size.reach + 3, 0:LANES]
    return parts[0:1] + parts[1:2] + parts[2:3]


def diagonal_kernel(size, out):
    place = lax.broadcasted_iota(jnp.int32, out.shape, 1)
    row = lax.broadcasted_iota(jnp.int32, out.shape, 0)
    chosen = (place == row) | (place == row + size.rows) | (place == row + 2 * size.rows)
    out[...] = jnp.where(chosen & (row < size.rows), 1.0, 0.0).astype(jnp.bfloat16)


def diagonals(size):
    return pl.pallas_call(
        functools.partial(diagonal_kernel, size),
        out_shape=jax.ShapeDtypeStruct((size.tall, 2 * LANES), jnp.bfloat16),
        out_specs=VMEM,
        compiler_params=pltpu.CompilerParams(vmem_limit_bytes=2 * MIB),
        cost_estimate=pl.CostEstimate(flops=10**10, bytes_accessed=10**6, transcendentals=0),
        name="diagonals",
    )()


def prepare_kernel(
    size, diagonal, scales, labels, moved, spread, wide, labels_only, split, lines
):
    frames, rows = size.frames, size.rows
    empty = jnp.zeros((frames, LANES), jnp.float32)

    def clear(e, carry):
        for t in range(size.tiles):
            moved[t, pl.ds(e * size.pitch, frames), :] = empty
            moved[t, pl.ds((e + rows) * size.pitch, frames), :] = empty
        return carry

    lax.fori_loop(0, 2 * size.reach, clear, 0, unroll=3)

    whole = scales[...]
    high = whole.astype(jnp.bfloat16).astype(jnp.float32)
    middle = (whole - high).astype(jnp.bfloat16).astype(jnp.float32)
    rest = jnp.zeros((frames, 2 * LANES - rows), jnp.float32)
    parts = [
        pltpu.roll(jnp.concatenate([part, rest], axis=1), k * rows, 1)
        for k, part in enumerate([high, middle, whole - high - middle])
    ]
    split[...] = parts[0] + parts[1] + parts[2]
    tall = size.tall
    group = 8
    ones = jnp.ones((2 * LANES, LANES), jnp.bfloat16)

    def spread_group(i, carry):
        chosen = []
        for j in range(group):
            line = split[pl.ds(i * group + j, 1), :]
            line = jnp.broadcast_to(line, (16, 2 * LANES)).astype(jnp.bfloat16)
            chosen.append(jnp.concatenate([line] * (tall // 16), axis=0) * diagonal[...])
        at = pl.multiple_of(i * (group * tall), 8)
        spread[pl.ds(at, group * tall), :] = jnp.dot(
            jnp.concatenate(chosen, axis=0), ones, preferred_element_type=jnp.float32
        )
        return carry

    lax.fori_loop(0, frames // group, spread_group, 0, unroll=8)
    wide[...] = widened(size, labels[...])
    top, bottom = wide[0 : size.reach, :], wide[rows - size.reach : rows, :]
    wanted = jnp.where(lax.axis_index("band") % 2 == 1, top, bottom)
    pack(size, labels_only, lines, wanted, jnp.zeros((1, LANES), jnp.float32))


def prepare(size, diagonal, scales, labels):
    return pl.pallas_call(
        functools.partial(prepare_kernel, size),
        out_shape=[
            jax.ShapeDtypeStruct((size.tiles, size.lines, LANES), jnp.float32),
            jax.ShapeDtypeStruct((size.frames * size.tall, LANES), jnp.float32),
            jax.ShapeDtypeStruct((size.rows, size.width), jnp.float32),
            jax.ShapeDtypeStruct((size.packed, size.width), jnp.bfloat16),
        ],
        in_specs=[VMEM] * 3,
        out_specs=[VMEM] * 4,
        scratch_shapes=[
            pltpu.VMEM((size.frames, 2 * LANES), jnp.float32),
            pltpu.VMEM((size.packed, size.width), jnp.float32),
        ],
        compiler_params=pltpu.CompilerParams(vmem_limit_bytes=8 * MIB),
        cost_estimate=pl.CostEstimate(flops=5 * 10**8, bytes_accessed=10**6, transcendentals=0),
        name="prepare",
    )(diagonal, scales, labels)


def shift_kernel(
    size, row_shift, col_shift, spread, codes, wide, cleared, moved, payload, total, lines
):
    frames, rows, cols, tiles, reach = size.frames, size.rows, size.cols, size.tiles, size.reach
    total[...] = jnp.zeros((rows, LANES), jnp.float32)
    whole_lane = lax.broadcasted_iota(jnp.int32, (rows, LANES), 1)
    lane = whole_lane.astype(jnp.float32).astype(jnp.bfloat16)
    source = lax.broadcasted_iota(jnp.int32, (rows, LANES), 0)
    band = lax.axis_index("band")
    zero = jnp.zeros((rows, LANES), jnp.bfloat16)

    def shift_frame(f, carry):
        down, right = row_shift[f], col_shift[f]
        turn = jnp.where(right < 0, right + LANES, right)
        left_end = jnp.where(right < 0, 0, turn).astype(jnp.float32).astype(jnp.bfloat16)
        right_start = jnp.where(right < 0, turn, LANES).astype(jnp.float32).astype(jnp.bfloat16)
        from_left = lane < left_end
        from_right = lane >= right_start
        scale_f = spread[pl.ds(pl.multiple_of(f * size.tall, 8), rows), :]
        turned = [zero]
        for t in range(tiles):
            upper = min(cols, (t + 1) * LANES)
            value = codes[f, :, t * LANES : upper].astype(jnp.float32)
            if upper < (t + 1) * LANES:
                fill = jnp.zeros((rows, (t + 1) * LANES - upper), jnp.float32)
                value = jnp.concatenate([value, fill], axis=1)
            turned.append(pltpu.roll((value * scale_f).astype(jnp.bfloat16), turn, 1))
        turned.append(zero)
        start = (reach + down) * size.pitch + f
        row_sum = jnp.zeros((rows, LANES), jnp.float32)
        for t in range(tiles):
            out = jnp.where(
                from_left, turned[t], jnp.where(from_right, turned[t + 2], turned[t + 1])
            ).astype(jnp.float32)
            moved[t, pl.ds(start, rows, stride=size.pitch), :] = out
            if (t + 1) * LANES > cols:
                out = jnp.where(whole_lane < cols - t * LANES, out, 0.0)
            row_sum = row_sum + out
        target = source + (band * rows + down)
        total[...] += jnp.where((target >= 0) & (target < cols), row_sum, 0.0)
        return carry

    lax.fori_loop(0, frames, shift_frame, 0, unroll=8)
    top, bottom = wide[0:reach, :], wide[rows - reach : rows, :]
    sums = jnp.sum(total[...], axis=0, keepdims=True)
    pack(size, payload, lines, jnp.where(band % 2 == 1, bottom, top), sums)


def shift_frames(size, row_shift, col_shift, spread, codes, wide, cleared):
    return pl.pallas_call(
        functools.partial(shift_kernel, size),
        out_shape=[
            jax.ShapeDtypeStruct(cleared.shape, jnp.float32),
            jax.ShapeDtypeStruct((size.packed, size.width), jnp.bfloat16),
        ],
        in_specs=[SMEM] * 2 + [VMEM] * 4,
        out_specs=[VMEM] * 2,
        scratch_shapes=[
            pltpu.VMEM((size.rows, LANES), jnp.float32),
            pltpu.VMEM((size.packed, size.width), jnp.float32),
        ],
        input_output_aliases={5: 0},
        compiler_params=pltpu.CompilerParams(vmem_limit_bytes=12 * MIB),
        cost_estimate=pl.CostEstimate(flops=6 * 10**9, bytes_accessed=10**6, transcendentals=0),
        name="shift",
    )(row_shift, col_shift, spread, codes, wide, cleared)


def table_consts(size):
    segment = lax.broadcasted_iota(jnp.int32, (16, size.width), 0)
    column = lax.broadcasted_iota(jnp.int32, (16, size.width), 1).astype(jnp.float32)
    xcoord = ((column + 0.5) / size.cols - 0.5).astype(jnp.bfloat16)
    ids = [
        (segment + 16 * k).astype(jnp.float32).astype(jnp.bfloat16) for k in range(SEGS // 16)
    ]
    return ids, xcoord


def add_row(size, consts, label_row, values, moments, e):
    ids, xcoord = consts
    zero = jnp.zeros((16, size.width), jnp.bfloat16)
    one = jnp.ones((16, size.width), jnp.bfloat16)
    label = jnp.broadcast_to(label_row, (16, size.width)).astype(jnp.bfloat16)
    plain, by_x = [], []
    for k in range(SEGS // 16):
        same = label == ids[k]
        plain.append(jnp.where(same, one, zero))
        by_x.append(jnp.where(same, xcoord, zero))
    table = jnp.concatenate(plain + by_x, axis=0)
    sums = lax.dot_general(
        table, values, (((1,), (1,)), ((), ())), preferred_element_type=jnp.float32
    )
    first_row = lax.axis_index("band") * size.rows
    offset = (first_row + e - size.reach).astype(jnp.float32)
    ycoord = ((offset + 0.5) / size.cols - 0.5).astype(jnp.bfloat16).astype(jnp.float32)
    moments[0:SEGS, :] += sums[0:SEGS]
    moments[SEGS : 2 * SEGS, :] += sums[0:SEGS] * ycoord
    moments[2 * SEGS : 3 * SEGS, :] += sums[SEGS : 2 * SEGS]


def values_of(size, moved, e):
    base = e * size.pitch
    tiles = [
        moved[t, pl.ds(base, size.frames), :].astype(jnp.bfloat16) for t in range(size.tiles)
    ]
    return jnp.concatenate(tiles, axis=1)


def core_kernel(size, first, last, started, moved, wide, token, *refs):
    if started:
        before, moments = refs
        moments[...] = before[...]
    else:
        (moments,) = refs
        moments[...] = jnp.zeros(moments.shape, jnp.float32)
    consts = table_consts(size)

    def step(r, carry):
        e = r + size.reach
        add_row(size, consts, wide[pl.ds(r, 1), :], values_of(size, moved, e), moments, e)
        return carry

    lax.fori_loop(first, last, step, 0, unroll=9)


def core_rows(size, moved, wide, token, before, first, last):
    args = [moved, wide, token] + ([] if before is None else [before])
    specs = [VMEM, VMEM, pl.BlockSpec(memory_space=pl.ANY)] + [VMEM] * (len(args) - 3)
    return pl.pallas_call(
        functools.partial(core_kernel, size, first, last, before is not None),
        out_shape=jax.ShapeDtypeStruct((3 * SEGS, size.frames), jnp.float32),
        in_specs=specs,
        out_specs=VMEM,
        compiler_params=pltpu.CompilerParams(vmem_limit_bytes=8 * MIB),
        cost_estimate=pl.CostEstimate(flops=4 * 10**9, bytes_accessed=10**6, transcendentals=0),
        name="core",
    )(*args)


def edge_kernel(size, moved, first_got, second_got, token, before, coeffs, send, wide, moments):
    frames, rows, reach = size.frames, size.rows, size.reach
    moments[...] = before[...]
    band, bands = lax.axis_index("band"), lax.axis_size("band")
    odd = band % 2 == 1
    first = first_got[...].astype(jnp.float32)[0:reach, :]
    second = second_got[...].astype(jnp.float32)[0:reach, :]
    wide[0:reach, :] = jnp.where(odd, second, first)
    wide[reach : 2 * reach, :] = jnp.where(odd, first, second)
    nothing = jnp.full((reach, size.width), -1.0, jnp.float32)

    @pl.when(band == 0)
    def _():
        wide[0:reach, :] = nothing

    @pl.when(band == bands - 1)
    def _():
        wide[reach : 2 * reach, :] = nothing

    consts = table_consts(size)

    def step(r, carry):
        e = jnp.where(r < reach, r, r + rows)
        add_row(size, consts, wide[pl.ds(r, 1), :], values_of(size, moved, e), moments, e)
        return carry

    lax.fori_loop(0, 2 * reach, step, 0, unroll=9)
    partial = jnp.dot(
        moments[...].T,
        coeffs[...],
        precision=lax.Precision.HIGHEST,
        preferred_element_type=jnp.float32,
    )
    half = frames // 2
    width = MASKS // bands
    per = LANES // width
    lane = lax.broadcasted_iota(jnp.int32, (half, LANES), 1)
    for b in range(bands):
        at = (b // per) * LANES
        low = partial[:half, at : at + LANES]
        high = partial[half:, at : at + LANES]
        if b % per == 0:
            high = pltpu.roll(high, width, 1)
        else:
            low = pltpu.roll(low, width, 1)
        send[b, 0:half, :] = jnp.where(lane < width, low, high)


def edge_rows(size, moved, first_got, second_got, token, before, coeffs):
    return pl.pallas_call(
        functools.partial(edge_kernel, size),
        out_shape=jax.ShapeDtypeStruct(
            (lax.axis_size("band"), size.frames // 2 + 8, LANES), jnp.float32
        ),
        in_specs=[VMEM, VMEM, VMEM, pl.BlockSpec(memory_space=pl.ANY), VMEM, VMEM],
        out_specs=VMEM,
        scratch_shapes=[
            pltpu.VMEM((2 * size.reach, size.width), jnp.float32),
            pltpu.VMEM((3 * SEGS, size.frames), jnp.float32),
        ],
        compiler_params=pltpu.CompilerParams(vmem_limit_bytes=12 * MIB),
        cost_estimate=pl.CostEstimate(flops=4 * 10**9, bytes_accessed=10**6, transcendentals=0),
        name="edge",
    )(moved, first_got, second_got, token, before, coeffs)


def first_join_kernel(size, own, other, token, out):
    out[...] = jnp.zeros(out.shape, jnp.float32)
    out[0:1, :] = packed_sums(size, own) + packed_sums(size, other)


def join_kernel(size, *refs):
    total = refs[0][...]
    for part in refs[1:-2]:
        total = total + part[...]
    refs[-1][...] = total


def join(size, kernel, parts, token):
    return pl.pallas_call(
        functools.partial(kernel, size),
        out_shape=jax.ShapeDtypeStruct((8, LANES), jnp.float32),
        in_specs=[VMEM] * len(parts) + [pl.BlockSpec(memory_space=pl.ANY)],
        out_specs=VMEM,
        compiler_params=pltpu.CompilerParams(vmem_limit_bytes=2 * MIB),
        name="join",
    )(*parts, token)


def put_kernel(send, own, other, out):
    bands, height, _ = out.shape
    for b in range(bands):
        out[b, height - 8 : height, :] = own[...] + other[...]


def put_total(send, own, other):
    return pl.pallas_call(
        put_kernel,
        out_shape=jax.ShapeDtypeStruct(send.shape, jnp.float32),
        in_specs=[VMEM] * 3,
        out_specs=VMEM,
        input_output_aliases={0: 0},
        compiler_params=pltpu.CompilerParams(vmem_limit_bytes=2 * MIB),
        name="put",
    )(send, own, other)


def finish_kernel(frame_total, blocks, out):
    bands, height, _ = blocks.shape
    half = height - 8
    summed = blocks[0]
    for b in range(1, bands):
        summed = summed + blocks[b]
    mean_total = jnp.sum(summed[half:, :]) / frame_total
    scaled = summed[:half] / mean_total
    width = out.shape[1]
    out[0:half, :] = scaled[:, :width]
    out[half:, :] = scaled[:, width:]


def finish(blocks, frame_count):
    half = frame_count // 2
    return pl.pallas_call(
        functools.partial(finish_kernel, float(frame_count * lax.axis_size("scan"))),
        out_shape=jax.ShapeDtypeStruct((2 * half, LANES // 2), jnp.float32),
        in_specs=[VMEM],
        out_specs=VMEM,
        compiler_params=pltpu.CompilerParams(vmem_limit_bytes=8 * MIB),
        name="finish",
    )(blocks)


def upper_pair(b):
    return b ^ 1


def lower_pair(b):
    return b if b in (0, lax.axis_size("band") - 1) else ((b + 1) ^ 1) - 1


def partner_steps():
    scans, bands = lax.axis_size("scan"), lax.axis_size("band")
    around = {0: 3, 1: 2, 2: 1, 3: 0}

    def x_around(s):
        return (s // 8) * 8 + around[s // 2 % 4] * 2 + s % 2

    def z_around(s):
        return around[s // 8] * 8 + s % 8

    def same(b):
        return b

    moves = [
        [(lambda s: s ^ 1, lower_pair)],
        [(lambda s: s ^ 4, same), (lambda s: s ^ 2, same), (x_around, same)],
        [(lambda s: s ^ 8, same)],
        [(z_around, same)],
    ]
    return [
        [
            [(s * bands + b, move(s) * bands + turn(b)) for s in range(scans) for b in range(bands)]
            for move, turn in step
        ]
        for step in moves
    ]


def body(frame_codes, row_scales, row_shift, col_shift, segment_labels, mask_coeffs):
    frame_count, band_height, det_cols = frame_codes.shape
    size = Sizes(frame_count, band_height, det_cols)
    cleared, spread, wide, labels_only = prepare(
        size, diagonals(size), row_scales, segment_labels
    )
    moved, total = shift_frames(size, row_shift, col_shift, spread, frame_codes, wide, cleared)
    coeffs = mask_coeffs.reshape(3 * SEGS, MASKS)
    pairs = [(b, upper_pair(b)) for b in range(lax.axis_size("band"))]
    second_got = lax.ppermute(labels_only, "band", pairs)
    steps = partner_steps()
    cuts = [0, band_height // 4, band_height * 5 // 8, band_height]
    moments, got = None, []
    for i, step in enumerate(steps):
        got.append([lax.ppermute(total, ("scan", "band"), pairs) for pairs in step])
        if i < len(steps) - 1:
            moments = core_rows(size, moved, wide, total, moments, cuts[i], cuts[i + 1])
            kernel = first_join_kernel if i == 0 else join_kernel
            total = join(size, kernel, [total] + got[i], moments)
    send = edge_rows(size, moved, got[0][0], second_got, total, moments, coeffs)
    send = put_total(send, total, got[-1][0])
    blocks = lax.all_to_all(send, "band", 0, 0)
    return finish(blocks, frame_count)


def solution(mesh):
    return jax.shard_map(
        body,
        mesh=mesh,
        in_specs=(
            P("scan", "band", None),
            P("scan", "band"),
            P("scan"),
            P("scan"),
            P("band", None),
            P(),
        ),
        out_specs=P("scan", "band"),
        check_vma=False,
    )
```
